32 devices in a mesh: region: 4 (over x, core), sub: 8 (over z, y).
Axes of the slice: x: 2, y: 2, z: 4, core: 2. Of those that a mesh axis runs over, the one named last changes fastest.
Arguments:
- features: bfloat16 [256, 128, 256], P(('region', 'sub')), may hold values from -30 to 30
- voxel_mask: int32 [256, 128], P(('region', 'sub')), may hold values 0 or 1
- counts: int32 [32], replicated, may hold values from 4 to 8, as said below
- neighbors: int32 [256, 27], P(('region', 'sub')), may hold values from -1 to 255, as said below
- w_first: bfloat16 [6912, 256], replicated, may hold values from -0.15625 to 0.15625
- w_second: bfloat16 [6912, 256], replicated, may hold values from -0.15625 to 0.15625
- gain_first: float32 [256], replicated, may hold values from 0.1 to 1.9
- bias_first: float32 [256], replicated, may hold values from -3 to 3
- gain_second: float32 [256], replicated, may hold values from 0.1 to 1.9
- bias_second: float32 [256], replicated, may hold values from -3 to 3
- cotangent: bfloat16 [256, 128, 256], P(('region', 'sub')), may hold values from -30 to 30
Outputs:
- output: bfloat16 [256, 128, 256], P(('region', 'sub'))
- grad_features: bfloat16 [256, 128, 256], P(('region', 'sub'))
The draws below stay inside these ranges and needn't reach their ends.
Inputs may be any that keep to these rules, and one draw needn't show every extreme that they name: `counts`: every device has at least one more live brick than 3; some device has 8 and some 3 + 1. `neighbors`: entry 13 of a live slot's row is the slot itself; a slot at or beyond its device's count has -1 in every entry. Slot b names slot c at offset o exactly when c names b at offset 26 - o. Every named slot is live and lies on the same device or on the device just before or just after it in the order of region+sub; a slot on the device after lies among that device's first 3 slots, a slot on the device before among its last 3 live slots.
All inputs are finite; a program needn't handle non-finite values. No bound on the sum of `voxel_mask` on one device may be relied on, other than what follows from the above.
Results may differ from the reference program's by a relative error of at most 0.003.
The reference program's roundings to bfloat16 on the way (of `act_first`, `hidden`, `act_second`, `grad_branch` and `grad_hidden`) count: a program that leaves them out, or rounds other values in their place, can miss the bound.
Values may be sent and summed in bfloat16 or wider, within the bound.
No kernel may reach another device: no remote copies, remote signals or barrier semaphores. Data moves between devices by JAX's collectives and lax.ppermute only.
A program may use at most 128 MiB of HBM per device.

```python
import math
import jax
import jax.numpy as jnp
from jax import lax

C = 256
VOX = 128
GC = 8
EDGE = 3
CAP = 8
BRICKS = 256


def live_layout(key):
    device_total = BRICKS // CAP
    count_key, shuffle_key = jax.random.split(jax.random.fold_in(key, 7))
    live_counts = jax.random.randint(count_key, (device_total,), EDGE + 1, CAP + 1)
    shuffled = jax.random.permutation(shuffle_key, device_total)
    live_counts = live_counts.at[shuffled[0]].set(CAP).at[shuffled[1]].set(EDGE + 1)
    return live_counts.astype(jnp.int32)


def draw_counts(key, part):
    return live_layout(key)


def slot_of(rank_values, starts):
    owner_device = jnp.sum((starts[None, None, :] <= rank_values[:, :, None]).astype(jnp.int32), axis=-1) - 1
    return owner_device * CAP + rank_values - starts[owner_device]


def draw_neighbors(key, part):
    live_counts = live_layout(key)
    reach_key, keep_key = jax.random.split(jax.random.fold_in(key, 11))
    starts = jnp.cumsum(live_counts) - live_counts
    live_total = jnp.sum(live_counts)
    slot_ids = jnp.arange(BRICKS, dtype=jnp.int32)
    owner_device = slot_ids // CAP
    alive_slot = slot_ids % CAP < live_counts[owner_device]
    live_rank = jnp.clip(starts[owner_device] + slot_ids % CAP, 0, BRICKS - 1)
    reach_steps = jax.random.randint(reach_key, (13,), 1, EDGE + 1).at[12].set(EDGE)
    keep_link = (jax.random.randint(keep_key, (BRICKS, 13), 0, 5) < 3).at[:, 12].set(True)
    upper_rank = live_rank[:, None] + reach_steps[None, :]
    lower_rank = live_rank[:, None] - reach_steps[None, :]
    upper_ok = alive_slot[:, None] & (upper_rank < live_total) & keep_link[live_rank]
    lower_keep = jnp.take_along_axis(keep_link, jnp.clip(lower_rank, 0, BRICKS - 1), axis=0)
    lower_ok = alive_slot[:, None] & (lower_rank >= 0) & lower_keep
    upper_ids = jnp.where(upper_ok, slot_of(jnp.clip(upper_rank, 0, live_total - 1), starts), -1)
    lower_ids = jnp.where(lower_ok, slot_of(jnp.clip(lower_rank, 0, live_total - 1), starts), -1)
    center_ids = jnp.where(alive_slot, slot_ids, -1)
    table = jnp.concatenate([lower_ids[:, ::-1], center_ids[:, None], upper_ids], axis=1)
    return table.astype(jnp.int32)


def device_levels(level_key, lowest, highest):
    device_total = BRICKS // CAP
    drawn = jax.random.uniform(level_key, (device_total,), jnp.float32, 0.0, math.log(highest / lowest))
    return jnp.repeat(lowest * jnp.exp(drawn), CAP)


def draw_features(key, part):
    noise_key = jax.random.fold_in(jax.random.fold_in(key, 3), 0)
    group_key = jax.random.fold_in(jax.random.fold_in(key, 3), 2)
    channel_key = jax.random.fold_in(jax.random.fold_in(key, 3), 3)
    level_key = jax.random.fold_in(jax.random.fold_in(key, 3), 4)
    brick_level = device_levels(level_key, 0.6, 4.5)
    group_level = jnp.clip(jax.random.normal(group_key, (C // GC,), jnp.float32), -1.5, 1.5)
    channel_level = 0.3 * jnp.clip(jax.random.normal(channel_key, (C,), jnp.float32), -2.0, 2.0)
    offset = jnp.repeat(group_level, GC) + channel_level
    values = jnp.clip(jax.random.normal(noise_key, (BRICKS, VOX, C), jnp.float32), -4.5, 4.5)
    values = values + offset[None, None, :]
    return (values * brick_level[:, None, None]).astype(jnp.bfloat16)


def draw_cotangent(key, part):
    noise_key, sign_key, group_key, channel_key, level_key = jax.random.split(jax.random.fold_in(key, 5), 5)
    brick_level = device_levels(level_key, 0.3, 3.0)
    group_level = 0.5 + jax.random.uniform(group_key, (C // GC,), jnp.float32, 0.0, 1.0)
    group_sign = jnp.where(jax.random.randint(sign_key, (C // GC,), 0, 2) == 0, -1.0, 1.0)
    channel_level = 0.2 * jnp.clip(jax.random.normal(channel_key, (C,), jnp.float32), -2.0, 2.0)
    offset = jnp.repeat(group_level * group_sign, GC) + channel_level
    values = 0.7 * jnp.clip(jax.random.normal(noise_key, (BRICKS, VOX, C), jnp.float32), -6.0, 6.0)
    values = values + offset[None, None, :]
    return (values * brick_level[:, None, None]).astype(jnp.bfloat16)


def place_ends(values, stream_key, least, high):
    extent = values.shape
    index_at = [jax.random.randint(jax.random.fold_in(stream_key, axis), (), 0, extent[axis]) for axis in range(len(extent))]
    values = values.at[tuple(index_at)].set(least)
    longest = extent.index(max(extent))
    index_at[longest] = (index_at[longest] + 1) % extent[longest]
    return values.at[tuple(index_at)].set(high)


def scatter_about(stream_key, extent, deviation, reach, kind=jnp.bfloat16):
    values = jax.random.normal(stream_key, extent, jnp.float32) * deviation
    return jnp.minimum(jnp.maximum(values, -reach), reach).astype(kind)


def setup_inputs(seed: int = 0) -> dict:
    key_of = jax.random.split(jax.random.key(seed), 12)
    features = draw_features(jax.random.fold_in(key_of[11], 71), 0)
    voxel_mask = place_ends((jax.random.randint(key_of[1], (BRICKS, VOX), 0, 4) < 3).astype(jnp.int32), jax.random.fold_in(key_of[1], 1), 0, 1)
    counts = draw_counts(jax.random.fold_in(key_of[11], 71), 0)
    neighbors = draw_neighbors(jax.random.fold_in(key_of[11], 71), 0)
    w_first = scatter_about(key_of[4], (27 * C, C), (27 * C // 4) ** -0.5, 0.15625)
    w_second = scatter_about(key_of[5], (27 * C, C), (27 * C // 4) ** -0.5, 0.15625)
    gain_first = jnp.clip(1.0 + 0.18 * jax.random.normal(key_of[6], (C,), jnp.float32), 0.1, 1.9)
    bias_first = scatter_about(key_of[7], (C,), 0.5, 3.0, jnp.float32)
    gain_second = jnp.clip(1.0 + 0.18 * jax.random.normal(key_of[8], (C,), jnp.float32), 0.1, 1.9)
    bias_second = scatter_about(key_of[9], (C,), 0.5, 3.0, jnp.float32)
    cotangent = draw_cotangent(jax.random.fold_in(key_of[11], 71), 0)
    return {"features": features, "voxel_mask": voxel_mask, "counts": counts, "neighbors": neighbors, "w_first": w_first, "w_second": w_second, "gain_first": gain_first, "bias_first": bias_first, "gain_second": gain_second, "bias_second": bias_second, "cotangent": cotangent}


eps_norm = 1e-05

def window_columns(brick_grid):
    number = brick_grid.shape[0]
    channels = brick_grid.shape[-1]
    padded_tile = brick_grid.reshape(number, 3, 3, 3, 4, 4, 8, channels)
    padded_tile = padded_tile.transpose(0, 1, 4, 2, 5, 3, 6, 7).reshape(number, 12, 12, 24, channels)
    padded_tile = padded_tile[:, 3:9, 3:9, 7:17]
    windows = [padded_tile[:, offset_x:offset_x + 4, offset_y:offset_y + 4, offset_z:offset_z + 8] for offset_x in range(3) for offset_y in range(3) for offset_z in range(3)]
    return jnp.stack(windows, axis=4).reshape(number * 128, 27 * channels)

def flipped(weights):
    channels = weights.shape[1]
    return weights.reshape(27, channels, channels)[::-1].transpose(0, 2, 1).reshape(27 * channels, channels)

def sparse_conv(activations, neighbors, weights):
    total_slots = activations.shape[0]
    source = jnp.concatenate([activations, jnp.zeros((1,) + activations.shape[1:], activations.dtype)], 0)
    safe_index = jnp.where(neighbors < 0, total_slots, neighbors).astype(jnp.int32)
    blocks = safe_index.reshape(-1, CAP, 27)

    def one_block(block_index):
        brick_grid = source[block_index]
        product = jnp.dot(window_columns(brick_grid), weights, preferred_element_type=jnp.float32)
        return product.reshape(CAP, 128, -1)
    return lax.map(one_block, blocks).reshape(total_slots, 128, -1)

def normalize(values, weight, gain_vec, bias_vec):
    grouped = values.reshape(values.shape[0], values.shape[1], -1, GC)
    group_weight = weight[:, :, None, None]
    voxel_total = jnp.sum(weight) * GC
    group_mean = lax.optimization_barrier(jnp.sum(grouped * group_weight, axis=(0, 1, 3))) / voxel_total
    centered = grouped - group_mean[None, None, :, None]
    spread = lax.optimization_barrier(jnp.sum(centered * centered * group_weight, axis=(0, 1, 3))) / voxel_total
    inv_scale = lax.rsqrt(spread + eps_norm)
    normed = (centered * inv_scale[None, None, :, None]).reshape(values.shape)
    return (normed * gain_vec + bias_vec, normed, inv_scale, voxel_total)

def norm_backward(grad_pre, normed, inv_scale, voxel_total, weight, gain_vec):
    shape_four = (grad_pre.shape[0], grad_pre.shape[1], -1, GC)
    scaled = (grad_pre * gain_vec).reshape(shape_four)
    normed_groups = normed.reshape(shape_four)
    group_weight = weight[:, :, None, None]
    first_sum = lax.optimization_barrier(jnp.sum(scaled * group_weight, axis=(0, 1, 3))) / voxel_total
    second = lax.optimization_barrier(jnp.sum(scaled * normed_groups * group_weight, axis=(0, 1, 3))) / voxel_total
    result = inv_scale[None, None, :, None] * (scaled - first_sum[None, None, :, None] - normed_groups * second[None, None, :, None])
    return result.reshape(grad_pre.shape)

def silu_slope(pre_values):
    sigmoid_part = jax.nn.sigmoid(pre_values)
    return sigmoid_part * (1.0 + pre_values * (1.0 - sigmoid_part))

def reference(features, voxel_mask, counts, neighbors, w_first, w_second, gain_first, bias_first, gain_second, bias_second, cotangent):
    alive_slot = (jnp.arange(CAP)[None, :] < counts[:, None]).reshape(-1)
    weight = voxel_mask.astype(jnp.float32) * alive_slot[:, None].astype(jnp.float32)
    weight_wide = weight[:, :, None]
    inputs = features.astype(jnp.float32) * weight_wide
    pre_first, normed_first, scale_first, voxel_total = normalize(inputs, weight, gain_first, bias_first)
    act_first = (jax.nn.silu(pre_first) * weight_wide).astype(jnp.bfloat16)
    hidden = (sparse_conv(act_first, neighbors, w_first) * weight_wide).astype(jnp.bfloat16)
    pre_second, normed_second, scale_second, voxel_total = normalize(hidden.astype(jnp.float32), weight, gain_second, bias_second)
    act_second = (jax.nn.silu(pre_second) * weight_wide).astype(jnp.bfloat16)
    branch = sparse_conv(act_second, neighbors, w_second)
    output = ((inputs + branch) * weight_wide).astype(jnp.bfloat16)
    grad_branch = (cotangent.astype(jnp.float32) * weight_wide).astype(jnp.bfloat16)
    grad_act_second = sparse_conv(grad_branch, neighbors, flipped(w_second))
    grad_pre_second = grad_act_second * silu_slope(pre_second) * weight_wide
    grad_hidden = (norm_backward(grad_pre_second, normed_second, scale_second, voxel_total, weight, gain_second) * weight_wide).astype(jnp.bfloat16)
    grad_act_first = sparse_conv(grad_hidden, neighbors, flipped(w_first))
    grad_pre_first = grad_act_first * silu_slope(pre_first) * weight_wide
    grad_inputs = norm_backward(grad_pre_first, normed_first, scale_first, voxel_total, weight, gain_first)
    grad_features = ((cotangent.astype(jnp.float32) + grad_inputs) * weight_wide).astype(jnp.bfloat16)
    return (output, grad_features)
```

```python
import functools

import jax
import jax.numpy as jnp
from jax import lax
from jax.experimental import pallas as pl
from jax.experimental.pallas import tpu as pltpu
from jax.sharding import PartitionSpec as P

GC = 8
EDGE = 3
AXES = ("region", "sub")
eps_norm = 1e-05
MARK = 2.0**100
MARK_LIMIT = 2.0**90
VMEM_LIMIT = 56 * 2**20
f32 = jnp.float32
bf16 = jnp.bfloat16


def vmem():
    return pl.BlockSpec(memory_space=pltpu.VMEM)


def smem():
    return pl.BlockSpec(memory_space=pltpu.SMEM)


def hbm():
    return pl.BlockSpec(memory_space=pl.ANY)


def call(kernel, name, in_specs, outs, scratch=()):
    return pl.pallas_call(
        kernel,
        name=name,
        in_specs=in_specs,
        out_specs=[vmem() for _ in outs],
        out_shape=[jax.ShapeDtypeStruct(*o) for o in outs],
        scratch_shapes=list(scratch),
        compiler_params=pltpu.CompilerParams(vmem_limit_bytes=VMEM_LIMIT),
    )


def lane_of(shape):
    return lax.broadcasted_iota(jnp.int32, shape, len(shape) - 1) % GC


def spread_first(x):
    x = jnp.where(lane_of(x.shape) == 0, x, 0.0)
    for s in (1, 2, 4):
        x = x + pltpu.roll(x, s, 1)
    return x


def group_total(x):
    for s in (1, 2, 4):
        x = x + pltpu.roll(x, 128 - s, 1)
    return spread_first(x)


def halves(x):
    return x[:, :128], x[:, 128:]


def pack_row(values):
    lane = lane_of((1, 128))
    row = jnp.zeros((1, 128), f32)
    for k, value in enumerate(values):
        row = jnp.where(lane == k, value, row)
    return row


def unpack_row(rows, k):
    return spread_first(pltpu.roll(rows, 128 - k, 1) if k else rows)


def join(pair):
    return jnp.concatenate(pair, axis=1)


def column_sum(x):
    return jnp.sum(x, axis=0, keepdims=True)


def moments_row(sum_row, count_row, second_pass):
    sums = [group_total(h) for h in halves(sum_row)]
    count = count_row * float(GC)
    safe = jnp.maximum(count, 1.0)
    mean = join([s / safe for s in sums])
    squares = [group_total(h) for h in halves(second_pass(mean))]
    return pack_row([sums[0], sums[1], squares[0], squares[1], count])


def combine_moments(rows):
    count = unpack_row(rows, 4)
    total = column_sum(count)
    safe = jnp.maximum(count, 1.0)
    means, scales = [], []
    for k in (0, 1):
        sums = unpack_row(rows, k)
        mean = column_sum(sums) / total
        apart = sums / safe - mean
        spread = column_sum(unpack_row(rows, 2 + k) + count * (apart * apart)) / total
        means.append(mean)
        scales.append(lax.rsqrt(spread + eps_norm))
    return join(means), join(scales), join([total, total])


def combine_pairs(rows, total):
    summed = column_sum(rows)
    first = join([unpack_row(summed, 0), unpack_row(summed, 1)]) / total
    second = join([unpack_row(summed, 2), unpack_row(summed, 3)]) / total
    return first, second


def pairs_row(first, second):
    return pack_row([group_total(h) for h in (*halves(first), *halves(second))])


def eight_rows(x):
    return jnp.sum(x.reshape(16, 8, x.shape[-1]), axis=0)


def put_slot(source, slot, values):
    tile = values.reshape(16, 8, 256)
    source[1, slot] = tile
    source[0, slot] = pltpu.roll(tile, 1, 1)
    source[2, slot] = pltpu.roll(tile, 7, 1)


def build(index, brick, source, windows):
    z = lax.broadcasted_iota(jnp.int32, (1, 8, 256), 1)
    for slab in range(6):
        dx, x = (0, 3) if slab == 0 else (2, 0) if slab == 5 else (1, slab - 1)
        for l in range(3):
            parts = []
            for dy, y, n in ((0, 3, 1), (1, 0, 4), (2, 0, 1)):
                at = pl.ds(x * 4 + y, n)
                part = source[l, index[brick, dx * 9 + dy * 3 + 1], at]
                if l != 1:
                    edge = source[l, index[brick, dx * 9 + dy * 3 + l], at]
                    part = jnp.where(z == (0 if l == 0 else 7), edge, part)
                parts.append(part)
            columns = jnp.concatenate(parts, axis=0)
            for j in range(3):
                windows[j * 3 + l, slab * 32 : slab * 32 + 32, :] = (
                    columns[j : j + 4].reshape(32, 256).astype(bf16)
                )


def product(windows, weights, backward):
    total = None
    for i in range(3):
        for j in range(3):
            for l in range(3):
                o = i * 9 + j * 3 + l
                taken = windows[j * 3 + l, i * 32 : i * 32 + 128, :]
                if backward:
                    part = lax.dot_general(
                        taken, weights[26 - o], (((1,), (1,)), ((), ())), preferred_element_type=f32
                    )
                else:
                    part = jnp.dot(taken, weights[o], preferred_element_type=f32)
                total = part if total is None else total + part
    return total


def conv(index, source, window_pair, weights, backward, capacity, finish, carry):
    even, odd = window_pair
    build(index, 0, source, even)

    def two(step, carry):
        first = 2 * step
        build(index, first + 1, source, odd)
        carry = finish(first, product(even, weights, backward), carry)
        build(index, jnp.minimum(first + 2, capacity - 1), source, even)
        return finish(first + 1, product(odd, weights, backward), carry)

    return lax.fori_loop(0, capacity // 2, two, carry)


def conv_scratch(slots):
    return [
        pltpu.VMEM((3, slots, 16, 8, 256), f32),
        pltpu.VMEM((9, 192, 256), bf16),
        pltpu.VMEM((9, 192, 256), bf16),
        pltpu.VMEM((27, 256, 256), bf16),
        pltpu.SemaphoreType.DMA,
    ]


def each_slot(own, before, after, body):
    capacity = own[0].shape[0]

    def run(refs, start, count):
        def step(k, _):
            body(refs, k, start + k)
            return 0

        lax.fori_loop(0, count, step, 0)

    run(own, 0, capacity)
    run(before, capacity, EDGE)
    run(after, capacity + EDGE, EDGE)


def sigmoid(x):
    return 1.0 / (1.0 + jnp.exp(-x))


def start_kernel(counts, features, mask, cotangent, row, marked, feat_up, feat_down, cot_up, cot_down):
    capacity = features.shape[0]
    live = counts[0]

    def first_pass(b, carry):
        total, count = carry
        wide = jnp.broadcast_to(mask[pl.ds(b, 1), :].astype(f32), (128, 128)).T
        wide = wide * jnp.where(b < live, 1.0, 0.0)
        values = features[b].astype(f32)
        on = join([wide, wide])
        marked[b] = jnp.where(on > 0.5, values, MARK).astype(bf16)
        return total + eight_rows(values * on), count + eight_rows(wide)

    total, count = lax.fori_loop(
        0, capacity, first_pass, (jnp.zeros((8, 256), f32), jnp.zeros((8, 128), f32))
    )
    for k in range(EDGE):
        up = live - EDGE + k
        feat_up[k] = marked[up]
        feat_down[k] = marked[k]
        cot_up[k] = jnp.where(marked[up].astype(f32) < MARK_LIMIT, cotangent[up].astype(f32), 0.0).astype(bf16)
        cot_down[k] = jnp.where(marked[k].astype(f32) < MARK_LIMIT, cotangent[k].astype(f32), 0.0).astype(bf16)

    def second_pass(mean):
        def step(b, carry):
            values = marked[b].astype(f32)
            apart = jnp.where(values < MARK_LIMIT, values - mean, 0.0)
            return carry + eight_rows(apart * apart)

        return column_sum(lax.fori_loop(0, capacity, step, jnp.zeros((8, 256), f32)))

    packed = moments_row(column_sum(total), column_sum(count), second_pass)
    row[...] = jnp.broadcast_to(packed, row.shape)


def grad_conv_kernel(
    index, counts, cotangent, marked, before, after, weights_hbm, grad, up, down, source, even, odd, weights, sem
):
    capacity = cotangent.shape[0]
    fetch = pltpu.make_async_copy(weights_hbm, weights, sem)
    fetch.start()

    def own_slot(b, _):
        values = cotangent[b].astype(f32)
        put_slot(source, b, jnp.where(marked[b].astype(f32) < MARK_LIMIT, values, 0.0))
        return 0

    lax.fori_loop(0, capacity, own_slot, 0)
    for k in range(EDGE):
        put_slot(source, capacity + k, before[k].astype(f32))
        put_slot(source, capacity + EDGE + k, after[k].astype(f32))
    put_slot(source, capacity + 2 * EDGE, jnp.zeros((128, 256), f32))
    fetch.wait()

    def finish(b, total, carry):
        grad[b] = total
        return carry

    conv(index, source, (even, odd), weights, True, capacity, finish, 0)
    for k in range(EDGE):
        up[k] = grad[counts[0] - EDGE + k].astype(bf16)
        down[k] = grad[k].astype(bf16)


def first_conv_kernel(
    index, counts, rows, marked, before, after, gain, bias, weights_hbm,
    hidden, row, up, down, stats, source, even, odd, weights, sem,
):
    capacity = marked.shape[0]
    fetch = pltpu.make_async_copy(weights_hbm, weights, sem)
    fetch.start()
    mean, inv_scale, voxel_total = combine_moments(rows[...])
    stats[...] = jnp.concatenate(
        [mean, inv_scale, voxel_total, jnp.zeros((5, 256), f32)], axis=0
    )
    slope = inv_scale * gain[...]
    shift = bias[...] - mean * slope

    def prepare(refs, k, slot):
        values = refs[0][k].astype(f32)
        pre = values * slope + shift
        put_slot(source, slot, jnp.where(values < MARK_LIMIT, pre * sigmoid(pre), 0.0))

    each_slot((marked,), (before,), (after,), prepare)
    put_slot(source, capacity + 2 * EDGE, jnp.zeros((128, 256), f32))
    fetch.wait()

    def finish(b, total, carry):
        sums, count = carry
        on = marked[b].astype(f32) < MARK_LIMIT
        rounded = total.astype(bf16).astype(f32)
        hidden[b] = jnp.where(on, rounded, MARK).astype(bf16)
        kept = jnp.where(on, rounded, 0.0)
        ones = jnp.where(on, 1.0, 0.0)
        return sums + eight_rows(kept), count + eight_rows(ones)

    sums, count = conv(
        index, source, (even, odd), weights, False, capacity, finish,
        (jnp.zeros((8, 256), f32), jnp.zeros((8, 256), f32)),
    )
    for k in range(EDGE):
        up[k] = hidden[counts[0] - EDGE + k]
        down[k] = hidden[k]

    def second_pass(mean):
        def step(b, carry):
            values = hidden[b].astype(f32)
            apart = jnp.where(values < MARK_LIMIT, values - mean, 0.0)
            return carry + eight_rows(apart * apart)

        return column_sum(lax.fori_loop(0, capacity, step, jnp.zeros((8, 256), f32)))

    packed = moments_row(column_sum(sums), column_sum(count)[:, :128], second_pass)
    row[...] = jnp.broadcast_to(packed, row.shape)


def slope_of(pre):
    part = sigmoid(pre)
    return part * (1.0 + pre * (1.0 - part))


def second_sums_kernel(rows, hidden, grad, gain, bias, row, stats):
    capacity = hidden.shape[0]
    mean, inv_scale, voxel_total = combine_moments(rows[...])
    stats[...] = jnp.concatenate(
        [mean, inv_scale, voxel_total, jnp.zeros((5, 256), f32)], axis=0
    )
    gains, biases = gain[...], bias[...]

    def step(b, carry):
        values = hidden[b].astype(f32)
        normed = (values - mean) * inv_scale
        scaled = grad[b] * slope_of(normed * gains + biases) * gains
        on = values < MARK_LIMIT
        scaled = jnp.where(on, scaled, 0.0)
        normed = jnp.where(on, normed, 0.0)
        return carry[0] + eight_rows(scaled), carry[1] + eight_rows(scaled * normed)

    zero = jnp.zeros((8, 256), f32)
    first, second = lax.fori_loop(0, capacity, step, (zero, zero))
    row[...] = jnp.broadcast_to(pairs_row(column_sum(first), column_sum(second)), row.shape)


def second_conv_kernel(
    index, hidden, before, after, stats, gain, bias, marked, weights_hbm,
    out, source, even, odd, weights, sem,
):
    capacity = hidden.shape[0]
    fetch = pltpu.make_async_copy(weights_hbm, weights, sem)
    fetch.start()
    slope = stats[1:2, :] * gain[...]
    shift = bias[...] - stats[0:1, :] * slope

    def prepare(refs, k, slot):
        values = refs[0][k].astype(f32)
        pre = values * slope + shift
        put_slot(source, slot, jnp.where(values < MARK_LIMIT, pre * sigmoid(pre), 0.0))

    each_slot((hidden,), (before,), (after,), prepare)
    put_slot(source, capacity + 2 * EDGE, jnp.zeros((128, 256), f32))
    fetch.wait()

    def finish(b, total, carry):
        inputs = marked[b].astype(f32)
        out[b] = jnp.where(inputs < MARK_LIMIT, inputs + total, 0.0).astype(bf16)
        return carry

    conv(index, source, (even, odd), weights, False, capacity, finish, 0)


def back_conv_kernel(
    index, rows, hidden, hid_before, hid_after, grad, grad_before, grad_after,
    stats_second, gain_second, bias_second, marked, stats_first, gain_first, bias_first, weights_hbm,
    scaled_out, row, source, even, odd, weights, sem,
):
    capacity = hidden.shape[0]
    fetch = pltpu.make_async_copy(weights_hbm, weights, sem)
    fetch.start()
    mean, inv_scale, voxel_total = (stats_second[k : k + 1, :] for k in range(3))
    first, second = combine_pairs(rows[...], voxel_total)
    gains, biases = gain_second[...], bias_second[...]

    def prepare(refs, k, slot):
        values = refs[0][k].astype(f32)
        normed = (values - mean) * inv_scale
        scaled = refs[1][k].astype(f32) * slope_of(normed * gains + biases) * gains
        result = inv_scale * (scaled - first - normed * second)
        put_slot(source, slot, jnp.where(values < MARK_LIMIT, result, 0.0))

    each_slot((hidden, grad), (hid_before, grad_before), (hid_after, grad_after), prepare)
    put_slot(source, capacity + 2 * EDGE, jnp.zeros((128, 256), f32))
    fetch.wait()
    mean_first, inv_first = stats_first[0:1, :], stats_first[1:2, :]
    gains_first, biases_first = gain_first[...], bias_first[...]

    def finish(b, total, carry):
        values = marked[b].astype(f32)
        normed = (values - mean_first) * inv_first
        on = values < MARK_LIMIT
        scaled = total * slope_of(normed * gains_first + biases_first) * gains_first
        scaled = jnp.where(on, scaled, 0.0)
        normed = jnp.where(on, normed, 0.0)
        scaled_out[b] = scaled
        return carry[0] + eight_rows(scaled), carry[1] + eight_rows(scaled * normed)

    zero = jnp.zeros((8, 256), f32)
    sums = conv(index, source, (even, odd), weights, True, capacity, finish, (zero, zero))
    row[...] = jnp.broadcast_to(pairs_row(column_sum(sums[0]), column_sum(sums[1])), row.shape)


def end_kernel(rows, scaled, marked, stats, cotangent, out):
    capacity = marked.shape[0]
    mean, inv_scale, voxel_total = (stats[k : k + 1, :] for k in range(3))
    first, second = combine_pairs(rows[...], voxel_total)

    def step(b, carry):
        values = marked[b].astype(f32)
        normed = (values - mean) * inv_scale
        result = cotangent[b].astype(f32) + inv_scale * (scaled[b] - first - normed * second)
        out[b] = jnp.where(values < MARK_LIMIT, result, 0.0).astype(bf16)
        return carry

    lax.fori_loop(0, capacity, step, 0)


def on_device(
    features, voxel_mask, counts, neighbors, w_first, w_second,
    gain_first, bias_first, gain_second, bias_second, cotangent,
):
    capacity, voxels, channels = features.shape
    devices = counts.shape[0]
    device = lax.axis_index(AXES)
    live = counts[device][None]
    live_before = counts[jnp.maximum(device - 1, 0)]

    owner = neighbors // capacity
    within = neighbors % capacity
    index = jnp.where(
        owner == device,
        within,
        jnp.where(
            owner == device - 1,
            capacity + within - (live_before - EDGE),
            capacity + EDGE + within,
        ),
    )
    index = jnp.where(neighbors < 0, capacity + 2 * EDGE, index).astype(jnp.int32)

    vectors = [v.reshape(1, channels) for v in (gain_first, bias_first, gain_second, bias_second)]
    gain_first, bias_first, gain_second, bias_second = vectors
    w_first = w_first.reshape(27, channels, channels)
    w_second = w_second.reshape(27, channels, channels)

    def shift_up(x):
        return lax.ppermute(x, AXES, [(i, i + 1) for i in range(devices - 1)])

    def shift_down(x):
        return lax.ppermute(x, AXES, [(i + 1, i) for i in range(devices - 1)])

    def exchange(row):
        return lax.all_to_all(row, AXES, 0, 0, tiled=True)

    whole = ((capacity, voxels, channels), bf16)
    whole_wide = ((capacity, voxels, channels), f32)
    edge = ((EDGE, voxels, channels), bf16)
    packed = ((devices, 128), f32)
    vector = ((8, channels), f32)
    slots = capacity + 2 * EDGE + 1

    row, marked, feat_up, feat_down, cot_up, cot_down = call(
        start_kernel, "start", [smem(), vmem(), vmem(), vmem()], [packed, whole, edge, edge, edge, edge]
    )(live, features, voxel_mask, cotangent)
    feat_before, feat_after = shift_up(feat_up), shift_down(feat_down)
    rows_first = exchange(row)

    hidden, row, hid_up, hid_down, stats_first = call(
        first_conv_kernel, "first_conv", [smem(), smem()] + [vmem()] * 6 + [hbm()],
        [whole, packed, edge, edge, vector], conv_scratch(slots),
    )(index, live, rows_first, marked, feat_before, feat_after, gain_first, bias_first, w_first)
    cot_before, cot_after = shift_up(cot_up), shift_down(cot_down)
    hid_before, hid_after = shift_up(hid_up), shift_down(hid_down)
    rows_second = exchange(row)

    grad, grad_up, grad_down = call(
        grad_conv_kernel, "grad_conv", [smem(), smem()] + [vmem()] * 4 + [hbm()],
        [whole_wide, edge, edge], conv_scratch(slots),
    )(index, live, cotangent, marked, cot_before, cot_after, w_second)
    grad_before, grad_after = shift_up(grad_up), shift_down(grad_down)

    row, stats_second = call(second_sums_kernel, "second_sums", [vmem()] * 5, [packed, vector])(
        rows_second, hidden, grad, gain_second, bias_second
    )
    rows_third = exchange(row)

    (output,) = call(
        second_conv_kernel, "second_conv", [smem()] + [vmem()] * 7 + [hbm()], [whole], conv_scratch(slots)
    )(index, hidden, hid_before, hid_after, stats_second, gain_second, bias_second, marked, w_second)

    scaled, row = call(
        back_conv_kernel, "back_conv", [smem()] + [vmem()] * 14 + [hbm()],
        [whole_wide, packed], conv_scratch(slots),
    )(
        index, rows_third, hidden, hid_before, hid_after, grad, grad_before, grad_after,
        stats_second, gain_second, bias_second, marked, stats_first, gain_first, bias_first, w_first,
    )
    rows_fourth = exchange(row)

    (grad_features,) = call(end_kernel, "end", [vmem()] * 5, [whole])(
        rows_fourth, scaled, marked, stats_first, cotangent
    )
    return (output, grad_features)


def solution(mesh):
    split = P(AXES, None, None)
    placed = (split, P(AXES, None), P(), P(AXES, None), P(), P(), P(), P(), P(), P(), split)
    return jax.shard_map(
        on_device, mesh=mesh, in_specs=placed, out_specs=(split, split), check_vma=False
    )
```

```python
import functools

import jax
import jax.numpy as jnp
from jax import lax
from jax.experimental import pallas as pl
from jax.experimental.pallas import tpu as pltpu
from jax.sharding import PartitionSpec as P

GC = 8
EDGE = 3
AXES = ("region", "sub")
eps_norm = 1e-05
MARK = 2.0**100
MARK_LIMIT = 2.0**90
VMEM_LIMIT = 20 * 2**20
COSTS = {"second_sums": 50, "second_conv": 8}
f32 = jnp.float32
bf16 = jnp.bfloat16


def vmem():
    return pl.BlockSpec(memory_space=pltpu.VMEM)


def smem():
    return pl.BlockSpec(memory_space=pltpu.SMEM)


def hbm():
    return pl.BlockSpec(memory_space=pltpu.HBM)


def call(kernel, name, in_specs, outs, scratch=()):
    made = pl.pallas_call(
        kernel,
        name=name,
        in_specs=in_specs,
        out_specs=[vmem() for _ in outs],
        out_shape=[jax.ShapeDtypeStruct(*o) for o in outs],
        scratch_shapes=list(scratch),
        cost_estimate=pl.CostEstimate(flops=int(COSTS[name] * 1.15e9), bytes_accessed=0, transcendentals=0)
        if name in COSTS
        else None,
        compiler_params=pltpu.CompilerParams(vmem_limit_bytes=VMEM_LIMIT),
    )

    def run(*operands):
        return made(
            *(
                pltpu.with_memory_space_constraint(x, pltpu.HBM)
                if spec.memory_space == pltpu.HBM
                else x
                for spec, x in zip(in_specs, operands)
            )
        )

    return run


class Fetched:
    def __init__(self, source, target, sem):
        self.copy = pltpu.make_async_copy(source, target, sem)
        self.copy.start()
        self.target = target

    def ready(self):
        self.copy.wait()
        return self.target


def lane_of(shape):
    return lax.broadcasted_iota(jnp.int32, shape, len(shape) - 1) % GC


def spread_first(x):
    x = jnp.where(lane_of(x.shape) == 0, x, 0.0)
    for s in (1, 2, 4):
        x = x + pltpu.roll(x, s, 1)
    return x


def group_total(x):
    for s in (1, 2, 4):
        x = x + pltpu.roll(x, 128 - s, 1)
    return spread_first(x)


def halves(x):
    return x[:, :128], x[:, 128:]


def pack_row(values):
    lane = lane_of((1, 128))
    row = jnp.zeros((1, 128), f32)
    for k, value in enumerate(values):
        row = jnp.where(lane == k, value, row)
    return row


def unpack_row(rows, k):
    return spread_first(pltpu.roll(rows, 128 - k, 1) if k else rows)


def join(pair):
    return jnp.concatenate(pair, axis=1)


def column_sum(x):
    return jnp.sum(x, axis=0, keepdims=True)


def moments_row(sum_row, count_row, second_pass):
    sums = [group_total(h) for h in halves(sum_row)]
    count = count_row * float(GC)
    safe = jnp.maximum(count, 1.0)
    mean = join([s / safe for s in sums])
    squares = [group_total(h) for h in halves(second_pass(mean))]
    return pack_row([sums[0], sums[1], squares[0], squares[1], count])


def combine_moments(rows):
    count = unpack_row(rows, 4)
    total = column_sum(count)
    safe = jnp.maximum(count, 1.0)
    means, scales = [], []
    for k in (0, 1):
        sums = unpack_row(rows, k)
        mean = column_sum(sums) / total
        apart = sums / safe - mean
        spread = column_sum(unpack_row(rows, 2 + k) + count * (apart * apart)) / total
        means.append(mean)
        scales.append(lax.rsqrt(spread + eps_norm))
    return join(means), join(scales), join([total, total])


def combine_pairs(rows, total):
    summed = column_sum(rows)
    first = join([unpack_row(summed, 0), unpack_row(summed, 1)]) / total
    second = join([unpack_row(summed, 2), unpack_row(summed, 3)]) / total
    return first, second


def pairs_row(first, second):
    return pack_row([group_total(h) for h in (*halves(first), *halves(second))])


def eight_rows(x):
    return jnp.sum(x.reshape(16, 8, x.shape[-1]), axis=0)


def put_slot(source, slot, values):
    tile = values.reshape(16, 8, 256)
    source[1, slot] = tile
    source[0, slot] = pltpu.roll(tile, 1, 1)
    source[2, slot] = pltpu.roll(tile, 7, 1)


def build(index, brick, source, windows):
    z = lax.broadcasted_iota(jnp.int32, (1, 8, 256), 1)
    for slab in range(6):
        dx, x = (0, 3) if slab == 0 else (2, 0) if slab == 5 else (1, slab - 1)
        for l in range(3):
            parts = []
            for dy, y, n in ((0, 3, 1), (1, 0, 4), (2, 0, 1)):
                at = pl.ds(x * 4 + y, n)
                part = source[l, index[brick, dx * 9 + dy * 3 + 1], at]
                if l != 1:
                    edge = source[l, index[brick, dx * 9 + dy * 3 + l], at]
                    part = jnp.where(z == (0 if l == 0 else 7), edge, part)
                parts.append(part)
            columns = jnp.concatenate(parts, axis=0)
            for j in range(3):
                windows[j * 3 + l, slab * 32 : slab * 32 + 32, :] = (
                    columns[j : j + 4].reshape(32, 256).astype(bf16)
                )


def product(pair, weights, backward):
    total = None
    for i in range(3):
        for j in range(3):
            for l in range(3):
                o = i * 9 + j * 3 + l
                taken = jnp.concatenate(
                    [pair[k, j * 3 + l, i * 32 : i * 32 + 128, :] for k in range(2)], axis=0
                )
                if backward:
                    part = lax.dot_general(
                        taken, weights[26 - o], (((1,), (1,)), ((), ())), preferred_element_type=f32
                    )
                else:
                    part = jnp.dot(taken, weights[o], preferred_element_type=f32)
                total = part if total is None else total + part
    return total


def conv(index, source, pairs, weights, backward, capacity, finish, carry):
    def build_pair(first, pair):
        first = jnp.minimum(first, capacity - 2)
        for k in range(2):
            build(index, first + k, source, pair.at[k])

    def finish_pair(first, pair, carry):
        both = product(pair, weights, backward)
        carry = finish(first, both[:128], carry)
        return finish(first + 1, both[128:], carry)

    even, odd = pairs
    build_pair(0, even)

    def four(step, carry):
        first = 4 * step
        build_pair(first + 2, odd)
        carry = finish_pair(first, even, carry)
        build_pair(first + 4, even)
        return finish_pair(first + 2, odd, carry)

    return lax.fori_loop(0, capacity // 4, four, carry)


def conv_scratch(slots):
    return [
        pltpu.VMEM((3, slots, 16, 8, 256), f32),
        pltpu.VMEM((2, 9, 192, 256), bf16),
        pltpu.VMEM((2, 9, 192, 256), bf16),
        pltpu.VMEM((27, 256, 256), bf16),
        pltpu.SemaphoreType.DMA,
    ]


def each_slot(capacity, own, before, after, body):
    def run(refs, start, count):
        def step(k, _):
            body(refs, k, start + k)
            return 0

        lax.fori_loop(0, count, step, 0)

    run(before, capacity, EDGE)
    run(after, capacity + EDGE, EDGE)
    run([x.ready() if isinstance(x, Fetched) else x for x in own], 0, capacity)


def sigmoid(x):
    return 1.0 / (1.0 + jnp.exp(-x))


def mark_kernel(
    counts, features, mask, gain_first, bias_first, gain_second, bias_second,
    marked, up, down, vectors, stage, mask_stage, vector_stage, feature_sem, small_sem,
):
    capacity = marked.shape[0]
    small = [pltpu.make_async_copy(mask, mask_stage, small_sem.at[0])]
    for k, vector in enumerate((gain_first, bias_first, gain_second, bias_second)):
        small.append(pltpu.make_async_copy(vector, vector_stage.at[k], small_sem.at[k + 1]))
    bricks = [
        pltpu.make_async_copy(features.at[b], stage.at[b], feature_sem.at[b]) for b in range(capacity)
    ]
    for copy in small + bricks:
        copy.start()
    live = counts[lax.axis_index(AXES)]
    small[0].wait()
    for b in range(capacity):
        wide = jnp.broadcast_to(mask_stage[b : b + 1, :].astype(f32), (128, 128)).T
        wide = wide * jnp.where(b < live, 1.0, 0.0)
        bricks[b].wait()
        marked[b] = jnp.where(join([wide, wide]) > 0.5, stage[b].astype(f32), MARK).astype(bf16)
    for k in range(EDGE):
        up[k] = marked[live - EDGE + k]
        down[k] = marked[k]
    for copy in small[1:]:
        copy.wait()
    for k in range(4):
        vectors[k : k + 1, :] = vector_stage[k]
    vectors[4:8, :] = jnp.zeros((4, 256), f32)


def first_sums_kernel(counts, marked_hbm, cotangent, row, up, down, stage, sems, marked, marked_sem):
    marked = Fetched(marked_hbm, marked, marked_sem)
    live = counts[lax.axis_index(AXES)]
    copies = []
    for k in range(EDGE):
        copies.append(pltpu.make_async_copy(cotangent.at[live - EDGE + k], stage.at[k], sems.at[k]))
        copies.append(pltpu.make_async_copy(cotangent.at[k], stage.at[EDGE + k], sems.at[EDGE + k]))
    for copy in copies:
        copy.start()
    marked = marked.ready()
    capacity = marked.shape[0]

    total = jnp.zeros((8, 256), f32)
    count = jnp.zeros((8, 128), f32)
    for b in range(capacity):
        values = marked[b].astype(f32)
        on = values < MARK_LIMIT
        total = total + eight_rows(jnp.where(on, values, 0.0))
        count = count + eight_rows(jnp.where(on[:, :128], 1.0, 0.0))

    def second_pass(mean):
        squares = jnp.zeros((8, 256), f32)
        for b in range(capacity):
            values = marked[b].astype(f32)
            apart = jnp.where(values < MARK_LIMIT, values - mean, 0.0)
            squares = squares + eight_rows(apart * apart)
        return column_sum(squares)

    packed = moments_row(column_sum(total), column_sum(count), second_pass)
    row[...] = jnp.broadcast_to(packed, row.shape)
    for copy in copies:
        copy.wait()
    for k in range(EDGE):
        for out, at, brick in ((up, k, live - EDGE + k), (down, EDGE + k, k)):
            on = marked[brick].astype(f32) < MARK_LIMIT
            out[k] = jnp.where(on, stage[at].astype(f32), 0.0).astype(bf16)


def grad_conv_kernel(
    index, counts, cotangent, marked_hbm, hidden, before, after, weights_hbm,
    grad, up, down, source, even, odd, weights, sem, stage, stage_sem, marked, marked_sem, edge_sem,
):
    capacity = marked.shape[0]
    live = counts[lax.axis_index(AXES)]
    edges = [
        pltpu.make_async_copy(hidden.at[pl.ds(live - EDGE, EDGE)], up.at[pl.ds(0, EDGE)], edge_sem.at[0]),
        pltpu.make_async_copy(hidden.at[pl.ds(0, EDGE)], down.at[pl.ds(0, EDGE)], edge_sem.at[1]),
    ]
    for copy in edges:
        copy.start()
    own = Fetched(cotangent, stage, stage_sem)
    marked = Fetched(marked_hbm, marked, marked_sem)
    fetch = pltpu.make_async_copy(weights_hbm, weights, sem)
    fetch.start()
    for k in range(EDGE):
        put_slot(source, capacity + k, before[k].astype(f32))
        put_slot(source, capacity + EDGE + k, after[k].astype(f32))
    put_slot(source, capacity + 2 * EDGE, jnp.zeros((128, 256), f32))
    marked, stage = marked.ready(), own.ready()

    def own_slot(b, _):
        values = stage[b].astype(f32)
        put_slot(source, b, jnp.where(marked[b].astype(f32) < MARK_LIMIT, values, 0.0))
        return 0

    lax.fori_loop(0, capacity, own_slot, 0)
    fetch.wait()

    def finish(b, total, carry):
        grad[b] = total
        return carry

    conv(index, source, (even, odd), weights, True, capacity, finish, 0)
    for copy in edges:
        copy.wait()
    for k in range(EDGE):
        up[EDGE + k] = grad[live - EDGE + k].astype(bf16)
        down[EDGE + k] = grad[k].astype(bf16)


def first_conv_kernel(
    index, rows, marked_hbm, before, after, vectors, weights_hbm,
    hidden, row, stats, source, even, odd, weights, sem, marked_stage, marked_sem,
):
    capacity = hidden.shape[0]
    marked = Fetched(marked_hbm, marked_stage, marked_sem)
    fetch = pltpu.make_async_copy(weights_hbm, weights, sem)
    fetch.start()
    mean, inv_scale, voxel_total = combine_moments(rows[...])
    stats[...] = jnp.concatenate(
        [mean, inv_scale, voxel_total, jnp.zeros((5, 256), f32)], axis=0
    )
    slope = inv_scale * vectors[0:1, :]
    shift = vectors[1:2, :] - mean * slope

    def prepare(refs, k, slot):
        values = refs[0][k].astype(f32)
        pre = values * slope + shift
        put_slot(source, slot, jnp.where(values < MARK_LIMIT, pre * sigmoid(pre), 0.0))

    each_slot(capacity, (marked,), (before,), (after,), prepare)
    put_slot(source, capacity + 2 * EDGE, jnp.zeros((128, 256), f32))
    fetch.wait()

    def finish(b, total, carry):
        sums, count = carry
        on = marked_stage[b].astype(f32) < MARK_LIMIT
        rounded = total.astype(bf16).astype(f32)
        hidden[b] = jnp.where(on, rounded, MARK).astype(bf16)
        kept = jnp.where(on, rounded, 0.0)
        ones = jnp.where(on, 1.0, 0.0)
        return sums + eight_rows(kept), count + eight_rows(ones)

    sums, count = conv(
        index, source, (even, odd), weights, False, capacity, finish,
        (jnp.zeros((8, 256), f32), jnp.zeros((8, 256), f32)),
    )
    def second_pass(mean):
        def step(b, carry):
            values = hidden[b].astype(f32)
            apart = jnp.where(values < MARK_LIMIT, values - mean, 0.0)
            return carry + eight_rows(apart * apart)

        return column_sum(lax.fori_loop(0, capacity, step, jnp.zeros((8, 256), f32)))

    packed = moments_row(column_sum(sums), column_sum(count)[:, :128], second_pass)
    row[...] = jnp.broadcast_to(packed, row.shape)


def slope_of(pre):
    part = sigmoid(pre)
    return part * (1.0 + pre * (1.0 - part))


def second_sums_kernel(rows, hidden_hbm, grad, vectors, row, stats, hidden, hidden_sem):
    capacity = hidden.shape[0]
    fetch = Fetched(hidden_hbm, hidden, hidden_sem)
    mean, inv_scale, voxel_total = combine_moments(rows[...])
    stats[...] = jnp.concatenate(
        [mean, inv_scale, voxel_total, jnp.zeros((5, 256), f32)], axis=0
    )
    gains, biases = vectors[2:3, :], vectors[3:4, :]

    def step(b, carry):
        values = hidden[b].astype(f32)
        normed = (values - mean) * inv_scale
        scaled = grad[b] * slope_of(normed * gains + biases) * gains
        on = values < MARK_LIMIT
        scaled = jnp.where(on, scaled, 0.0)
        normed = jnp.where(on, normed, 0.0)
        return carry[0] + eight_rows(scaled), carry[1] + eight_rows(scaled * normed)

    zero = jnp.zeros((8, 256), f32)
    fetch.ready()
    first, second = lax.fori_loop(0, capacity, step, (zero, zero), unroll=2)
    row[...] = jnp.broadcast_to(pairs_row(column_sum(first), column_sum(second)), row.shape)


def second_conv_kernel(
    index, hidden_hbm, before, after, stats, vectors, marked_hbm, weights_hbm,
    out, source, even, odd, weights, sem, hidden_stage, hidden_sem, marked, marked_sem,
):
    capacity = marked.shape[0]
    hidden = Fetched(hidden_hbm, hidden_stage, hidden_sem)
    marking = Fetched(marked_hbm, marked, marked_sem)
    fetch = pltpu.make_async_copy(weights_hbm, weights, sem)
    fetch.start()
    slope = stats[1:2, :] * vectors[2:3, :]
    shift = vectors[3:4, :] - stats[0:1, :] * slope

    def prepare(refs, k, slot):
        values = refs[0][k].astype(f32)
        pre = values * slope + shift
        put_slot(source, slot, jnp.where(values < MARK_LIMIT, pre * sigmoid(pre), 0.0))

    each_slot(capacity, (hidden,), (before,), (after,), prepare)
    put_slot(source, capacity + 2 * EDGE, jnp.zeros((128, 256), f32))
    marking.ready()
    fetch.wait()

    def finish(b, total, carry):
        inputs = marked[b].astype(f32)
        out[b] = jnp.where(inputs < MARK_LIMIT, inputs + total, 0.0).astype(bf16)
        return carry

    conv(index, source, (even, odd), weights, False, capacity, finish, 0)


def back_conv_kernel(
    index, rows, hidden_hbm, grad, before, after,
    stats_second, marked_hbm, stats_first, vectors, weights_hbm,
    scaled_out, row, source, even, odd, weights, sem, hidden_stage, hidden_sem, marked, marked_sem,
):
    capacity = marked.shape[0]
    hidden = Fetched(hidden_hbm, hidden_stage, hidden_sem)
    marking = Fetched(marked_hbm, marked, marked_sem)
    fetch = pltpu.make_async_copy(weights_hbm, weights, sem)
    fetch.start()
    mean, inv_scale, voxel_total = (stats_second[k : k + 1, :] for k in range(3))
    first, second = combine_pairs(rows[...], voxel_total)
    gains, biases = vectors[2:3, :], vectors[3:4, :]

    def prepare(refs, k, slot):
        values = refs[0][k].astype(f32)
        normed = (values - mean) * inv_scale
        scaled = refs[1][k].astype(f32) * slope_of(normed * gains + biases) * gains
        result = inv_scale * (scaled - first - normed * second)
        put_slot(source, slot, jnp.where(values < MARK_LIMIT, result, 0.0))

    halo = [(x.at[pl.ds(0, EDGE)], x.at[pl.ds(EDGE, EDGE)]) for x in (before, after)]
    each_slot(capacity, (hidden, grad), *halo, prepare)
    put_slot(source, capacity + 2 * EDGE, jnp.zeros((128, 256), f32))
    marking.ready()
    fetch.wait()
    mean_first, inv_first = stats_first[0:1, :], stats_first[1:2, :]
    gains_first, biases_first = vectors[0:1, :], vectors[1:2, :]

    def finish(b, total, carry):
        values = marked[b].astype(f32)
        normed = (values - mean_first) * inv_first
        on = values < MARK_LIMIT
        scaled = total * slope_of(normed * gains_first + biases_first) * gains_first
        scaled = jnp.where(on, scaled, 0.0)
        normed = jnp.where(on, normed, 0.0)
        scaled_out[b] = scaled
        return carry[0] + eight_rows(scaled), carry[1] + eight_rows(scaled * normed)

    zero = jnp.zeros((8, 256), f32)
    sums = conv(index, source, (even, odd), weights, True, capacity, finish, (zero, zero))
    row[...] = jnp.broadcast_to(pairs_row(column_sum(sums[0]), column_sum(sums[1])), row.shape)


def end_kernel(rows, scaled, marked_hbm, stats, cotangent, out, stage, sem, marked, marked_sem):
    capacity = marked.shape[0]
    own = Fetched(cotangent, stage, sem)
    marking = Fetched(marked_hbm, marked, marked_sem)
    mean, inv_scale, voxel_total = (stats[k : k + 1, :] for k in range(3))
    first, second = combine_pairs(rows[...], voxel_total)
    own.ready()
    marking.ready()

    def step(b, carry):
        values = marked[b].astype(f32)
        normed = (values - mean) * inv_scale
        result = stage[b].astype(f32) + inv_scale * (scaled[b] - first - normed * second)
        out[b] = jnp.where(values < MARK_LIMIT, result, 0.0).astype(bf16)
        return carry

    lax.fori_loop(0, capacity, step, 0, unroll=2)


def on_device(
    features, voxel_mask, counts, neighbors, w_first, w_second,
    gain_first, bias_first, gain_second, bias_second, cotangent,
):
    capacity, voxels, channels = features.shape
    devices = counts.shape[0]
    device = lax.axis_index(AXES)
    live_before = counts[jnp.maximum(device - 1, 0)]

    owner = neighbors // capacity
    within = neighbors % capacity
    index = jnp.where(
        owner == device,
        within,
        jnp.where(
            owner == device - 1,
            capacity + within - (live_before - EDGE),
            capacity + EDGE + within,
        ),
    )
    index = jnp.where(neighbors < 0, capacity + 2 * EDGE, index).astype(jnp.int32)

    vectors = [v.reshape(1, channels) for v in (gain_first, bias_first, gain_second, bias_second)]
    gain_first, bias_first, gain_second, bias_second = vectors
    w_first = w_first.reshape(27, channels, channels)
    w_second = w_second.reshape(27, channels, channels)

    def shift_up(x):
        return lax.ppermute(x, AXES, [(i, (i + 1) % devices) for i in range(devices)])

    def shift_down(x):
        return lax.ppermute(x, AXES, [((i + 1) % devices, i) for i in range(devices)])

    def exchange(row):
        return lax.all_to_all(row, AXES, 0, 0, tiled=True)

    whole = ((capacity, voxels, channels), bf16)
    whole_wide = ((capacity, voxels, channels), f32)
    two_edges = ((2 * EDGE, voxels, channels), bf16)
    edge = ((EDGE, voxels, channels), bf16)
    packed = ((devices, 128), f32)
    vector = ((8, channels), f32)
    slots = capacity + 2 * EDGE + 1

    dma = pltpu.SemaphoreType.DMA
    marked, feat_up, feat_down, vectors = call(
        mark_kernel, "mark", [smem()] + [hbm()] * 6, [whole, edge, edge, vector],
        [
            pltpu.VMEM(*whole), pltpu.VMEM((capacity, voxels), jnp.int32),
            pltpu.VMEM((4, 1, channels), f32),
            dma((capacity,)), dma((5,)),
        ],
    )(counts, features, voxel_mask, gain_first, bias_first, gain_second, bias_second)
    feat_before, feat_after = shift_up(feat_up), shift_down(feat_down)
    row, cot_up, cot_down = call(
        first_sums_kernel, "first_sums", [smem(), hbm(), hbm()], [packed, edge, edge],
        [pltpu.VMEM((2 * EDGE, voxels, channels), bf16), dma((2 * EDGE,)), pltpu.VMEM(*whole), dma],
    )(counts, marked, cotangent)
    rows_first = exchange(row)
    cot_before, cot_after = shift_up(cot_up), shift_down(cot_down)

    hidden, row, stats_first = call(
        first_conv_kernel, "first_conv", [smem(), vmem(), hbm(), vmem(), vmem(), vmem(), hbm()],
        [whole, packed, vector], conv_scratch(slots) + [pltpu.VMEM(*whole), dma],
    )(index, rows_first, marked, feat_before, feat_after, vectors, w_first)
    rows_second = exchange(row)

    grad, up, down = call(
        grad_conv_kernel, "grad_conv", [smem(), smem(), hbm(), hbm(), hbm(), vmem(), vmem(), hbm()],
        [whole_wide, two_edges, two_edges],
        conv_scratch(slots) + [pltpu.VMEM(*whole), dma, pltpu.VMEM(*whole), dma, dma((2,))],
    )(index, counts, cotangent, marked, hidden, cot_before, cot_after, w_second)
    before, after = shift_up(up), shift_down(down)

    row, stats_second = call(
        second_sums_kernel, "second_sums", [vmem(), hbm(), vmem(), vmem()], [packed, vector],
        [pltpu.VMEM(*whole), dma],
    )(rows_second, hidden, grad, vectors)
    rows_third = exchange(row)

    (output,) = call(
        second_conv_kernel, "second_conv", [smem(), hbm(), vmem(), vmem(), vmem(), vmem(), hbm(), hbm()],
        [whole],
        conv_scratch(slots) + [pltpu.VMEM(*whole), dma, pltpu.VMEM(*whole), dma],
    )(index, hidden, before, after, stats_second, vectors, marked, w_second)

    scaled, row = call(
        back_conv_kernel, "back_conv", [smem(), vmem(), hbm()] + [vmem()] * 4 + [hbm(), vmem(), vmem(), hbm()],
        [whole_wide, packed],
        conv_scratch(slots) + [pltpu.VMEM(*whole), dma, pltpu.VMEM(*whole), dma],
    )(
        index, rows_third, hidden, grad, before, after,
        stats_second, marked, stats_first, vectors, w_first,
    )
    rows_fourth = exchange(row)

    (grad_features,) = call(
        end_kernel, "end", [vmem(), vmem(), hbm(), vmem(), hbm()], [whole],
        [pltpu.VMEM(*whole), dma, pltpu.VMEM(*whole), dma],
    )(rows_fourth, scaled, marked, stats_first, cotangent)
    return (output, grad_features)


def solution(mesh):
    split = P(AXES, None, None)
    placed = (split, P(AXES, None), P(), P(AXES, None), P(), P(), P(), P(), P(), P(), split)
    return jax.shard_map(
        on_device, mesh=mesh, in_specs=placed, out_specs=(split, split), check_vma=False
    )
```

```python
import functools

import jax
import jax.numpy as jnp
from jax import lax
from jax.experimental import pallas as pl
from jax.experimental.pallas import tpu as pltpu
from jax.sharding import PartitionSpec as P

GC = 8
EDGE = 3
AXES = ("region", "sub")
eps_norm = 1e-05
MARK = 2.0**100
MARK_LIMIT = 2.0**90
VMEM_LIMIT = 20 * 2**20
COSTS = {"second_sums": 50, "second_conv": 8, "first_conv": 8}
f32 = jnp.float32
bf16 = jnp.bfloat16


def vmem():
    return pl.BlockSpec(memory_space=pltpu.VMEM)


def hbm():
    return pl.BlockSpec(memory_space=pltpu.HBM)


def call(kernel, name, in_specs, outs, scratch=()):
    made = pl.pallas_call(
        kernel,
        name=name,
        in_specs=in_specs,
        out_specs=[hbm() if len(o) == 3 else vmem() for o in outs],
        out_shape=[pltpu.HBM(*o[:2]) if len(o) == 3 else jax.ShapeDtypeStruct(*o) for o in outs],
        scratch_shapes=list(scratch),
        cost_estimate=pl.CostEstimate(flops=int(COSTS[name] * 1.15e9), bytes_accessed=0, transcendentals=0)
        if name in COSTS
        else None,
        compiler_params=pltpu.CompilerParams(vmem_limit_bytes=VMEM_LIMIT),
    )

    def run(*operands):
        return made(
            *(
                pltpu.with_memory_space_constraint(x, pltpu.HBM)
                if spec.memory_space == pltpu.HBM
                else x
                for spec, x in zip(in_specs, operands)
            )
        )

    return run


class Fetched:
    def __init__(self, source, target, sem):
        self.copy = pltpu.make_async_copy(source, target, sem)
        self.copy.start()
        self.target = target

    def ready(self):
        self.copy.wait()
        return self.target


def lane_of(shape):
    return lax.broadcasted_iota(jnp.int32, shape, len(shape) - 1) % GC


def spread_first(x):
    x = jnp.where(lane_of(x.shape) == 0, x, 0.0)
    for s in (1, 2, 4):
        x = x + pltpu.roll(x, s, 1)
    return x


def group_total(x):
    for s in (1, 2, 4):
        x = x + pltpu.roll(x, 128 - s, 1)
    return spread_first(x)


def halves(x):
    return x[:, :128], x[:, 128:]


def pack_row(values):
    lane = lane_of((1, 128))
    row = jnp.zeros((1, 128), f32)
    for k, value in enumerate(values):
        row = jnp.where(lane == k, value, row)
    return row


def unpack_row(rows, k):
    return spread_first(pltpu.roll(rows, 128 - k, 1) if k else rows)


def join(pair):
    return jnp.concatenate(pair, axis=1)


def column_sum(x):
    return jnp.sum(x, axis=0, keepdims=True)


def no_moments():
    zero = jnp.zeros((8, 256), f32)
    return zero, zero, zero, zero[:, :128]


def add_moments(moments, values, on, first):
    base, sums, squares, count = moments
    here = eight_rows(jnp.where(on[:, :128], 1.0, 0.0))
    number = jnp.maximum(here, 1.0)
    base = jnp.where(first, eight_rows(jnp.where(on, values, 0.0)) / join([number, number]), base)
    apart = jnp.where(on.reshape(16, 8, 256), values.reshape(16, 8, 256) - base, 0.0)
    sums = sums + jnp.sum(apart, axis=0)
    squares = squares + jnp.sum(apart * apart, axis=0)
    return base, sums, squares, count + here


def moments_row(moments):
    base, total, square, count = moments
    safe = jnp.maximum(count, 1.0)
    number = column_sum(count)
    sums, squares = [], []
    for base, total, square in zip(halves(base), halves(total), halves(square)):
        apart = total / safe
        mean = base + apart
        group_sum = group_total(column_sum(count * mean))
        group_mean = group_sum / jnp.maximum(number * float(GC), 1.0)
        about = square - total * apart + count * ((mean - group_mean) * (mean - group_mean))
        sums.append(group_sum)
        squares.append(group_total(column_sum(about)))
    return pack_row([*sums, *squares, number * float(GC)])


def combine_moments(rows):
    count = unpack_row(rows, 4)
    total = column_sum(count)
    safe = jnp.maximum(count, 1.0)
    means, scales = [], []
    for k in (0, 1):
        sums = unpack_row(rows, k)
        mean = column_sum(sums) / total
        apart = sums / safe - mean
        spread = column_sum(unpack_row(rows, 2 + k) + count * (apart * apart)) / total
        means.append(mean)
        scales.append(lax.rsqrt(spread + eps_norm))
    return join(means), join(scales), join([total, total])


def combine_pairs(rows, total):
    summed = column_sum(rows)
    first = join([unpack_row(summed, 0), unpack_row(summed, 1)]) / total
    second = join([unpack_row(summed, 2), unpack_row(summed, 3)]) / total
    return first, second


def pairs_row(first, second):
    return pack_row([group_total(h) for h in (*halves(first), *halves(second))])


def eight_rows(x):
    return jnp.sum(x.reshape(16, 8, x.shape[-1]), axis=0)


def put_slot(source, slot, values):
    tile = values.reshape(16, 8, 256)
    source[1, slot] = tile
    source[0, slot] = pltpu.roll(tile, 1, 1)
    source[2, slot] = pltpu.roll(tile, 7, 1)


def build(index, brick, source, windows):
    z = lax.broadcasted_iota(jnp.int32, (1, 8, 256), 1)
    for slab in range(6):
        dx, x = (0, 3) if slab == 0 else (2, 0) if slab == 5 else (1, slab - 1)
        for l in range(3):
            parts = []
            for dy, y, n in ((0, 3, 1), (1, 0, 4), (2, 0, 1)):
                at = pl.ds(x * 4 + y, n)
                part = source[l, index[brick, dx * 9 + dy * 3 + 1], at]
                if l != 1:
                    edge = source[l, index[brick, dx * 9 + dy * 3 + l], at]
                    part = jnp.where(z == (0 if l == 0 else 7), edge, part)
                parts.append(part)
            columns = jnp.concatenate(parts, axis=0)
            for j in range(3):
                windows[j * 3 + l, slab * 32 : slab * 32 + 32, :] = (
                    columns[j : j + 4].reshape(32, 256).astype(bf16)
                )


def product(pair, weights, backward):
    total = None
    for i in range(3):
        for j in range(3):
            for l in range(3):
                o = i * 9 + j * 3 + l
                taken = jnp.concatenate(
                    [pair[k, j * 3 + l, i * 32 : i * 32 + 128, :] for k in range(2)], axis=0
                )
                if backward:
                    part = lax.dot_general(
                        taken, weights[26 - o], (((1,), (1,)), ((), ())), preferred_element_type=f32
                    )
                else:
                    part = jnp.dot(taken, weights[o], preferred_element_type=f32)
                total = part if total is None else total + part
    return total


def conv(index, source, pair, weights, backward, capacity, finish, carry):
    def two(step, carry):
        first = 2 * step
        for k in range(2):
            build(index, first + k, source, pair.at[k])
        both = product(pair, weights, backward)
        carry = finish(first, both[:128], carry)
        return finish(first + 1, both[128:], carry)

    return lax.fori_loop(0, capacity // 2, two, carry)


def conv_scratch(slots, capacity):
    return [
        pltpu.VMEM((3, slots, 16, 8, 256), f32),
        pltpu.VMEM((2, 9, 192, 256), bf16),
        pltpu.VMEM((27, 256, 256), bf16),
        pltpu.SemaphoreType.DMA,
        pltpu.SMEM((capacity, 27), jnp.int32),
        pltpu.SemaphoreType.DMA,
    ]


def each_slot(capacity, own, before, after, body):
    def run(refs, start, count):
        def step(k, _):
            body(refs, k, start + k)
            return 0

        lax.fori_loop(0, count, step, 0)

    run(before, capacity, EDGE)
    run(after, capacity + EDGE, EDGE)
    run([x.ready() if isinstance(x, Fetched) else x for x in own], 0, capacity)


def sigmoid(x):
    return 1.0 / (1.0 + jnp.exp(-x))


def mark_kernel(
    counts_hbm, features, mask, cotangent, gain_first, bias_first, gain_second, bias_second,
    marked_hbm, marked, feat_up, feat_down, cot_up, cot_down, vectors,
    stage, cot_stage, cot_sem, mask_stage, vector_stage, feature_sem, small_sem, counts, counts_sem, out_sem,
):
    capacity = marked.shape[0]
    counting = Fetched(counts_hbm, counts, counts_sem)
    small = [pltpu.make_async_copy(mask, mask_stage, small_sem.at[0])]
    for k, vector in enumerate((gain_first, bias_first, gain_second, bias_second)):
        small.append(pltpu.make_async_copy(vector, vector_stage.at[k], small_sem.at[k + 1]))

    def arriving(b):
        return pltpu.make_async_copy(features.at[b], stage.at[b], feature_sem.at[b])

    def kept(b):
        return pltpu.make_async_copy(marked.at[b], marked_hbm.at[b], out_sem.at[b])

    for copy in small + [arriving(b) for b in range(capacity)]:
        copy.start()
    live = counting.ready()[lax.axis_index(AXES)]
    edges = []
    for k in range(EDGE):
        for at, brick in ((k, live - EDGE + k), (EDGE + k, k)):
            edges.append(pltpu.make_async_copy(cotangent.at[brick], cot_stage.at[at], cot_sem.at[at]))
    for copy in edges:
        copy.start()
    small[0].wait()
    def step(b, _):
        wide = jnp.broadcast_to(mask_stage[pl.ds(b, 1), :].astype(f32), (128, 128)).T
        wide = wide * jnp.where(b < live, 1.0, 0.0)
        arriving(b).wait()
        marked[b] = jnp.where(join([wide, wide]) > 0.5, stage[b].astype(f32), MARK).astype(bf16)
        kept(b).start()
        return 0

    lax.fori_loop(0, capacity, step, 0, unroll=4)
    for copy in edges:
        copy.wait()
    for k in range(EDGE):
        for feat, cot, at, brick in (
            (feat_up, cot_up, k, live - EDGE + k), (feat_down, cot_down, EDGE + k, k)
        ):
            values = marked[brick]
            feat[k] = values
            on = values.astype(f32) < MARK_LIMIT
            cot[k] = jnp.where(on, cot_stage[at].astype(f32), 0.0).astype(bf16)
    for copy in small[1:] + [kept(b) for b in range(capacity)]:
        copy.wait()
    for k in range(4):
        vectors[k : k + 1, :] = vector_stage[k]
    vectors[4:8, :] = jnp.zeros((4, 256), f32)


def first_sums_kernel(
    counts_hbm, marked, neighbors_hbm, row, index_hbm,
    counts, counts_sem, neighbors, neighbors_sem, index, index_sem,
):
    counting = Fetched(counts_hbm, counts, counts_sem)
    naming = Fetched(neighbors_hbm, neighbors, neighbors_sem)
    device = lax.axis_index(AXES)
    counting.ready()

    capacity = marked.shape[0]
    live_before = counts[jnp.maximum(device - 1, 0)]
    named = naming.ready()[...]
    owner = lax.div(named, capacity)
    within = named - owner * capacity
    slot = jnp.where(
        owner == device,
        within,
        jnp.where(
            owner == device - 1, within + (capacity + EDGE - live_before), within + (capacity + EDGE)
        ),
    )
    index[...] = jnp.where(named < 0, capacity + 2 * EDGE, slot)
    indexed = pltpu.make_async_copy(index, index_hbm, index_sem)
    indexed.start()


    def step(b, moments):
        values = marked[b].astype(f32)
        return add_moments(moments, values, values < MARK_LIMIT, b == 0)

    moments = lax.fori_loop(0, capacity, step, no_moments(), unroll=2)
    row[...] = jnp.broadcast_to(moments_row(moments), row.shape)
    indexed.wait()


def grad_conv_kernel(
    index_hbm, cotangent, marked_hbm, before, after, weights_hbm,
    grad, source, windows, weights, sem, index, index_sem, stage, stage_sem, marked, marked_sem,
):
    capacity = marked.shape[0]
    indexing = Fetched(index_hbm, index, index_sem)
    own = Fetched(cotangent, stage, stage_sem)
    marked = Fetched(marked_hbm, marked, marked_sem)
    fetch = pltpu.make_async_copy(weights_hbm, weights, sem)
    fetch.start()
    for k in range(EDGE):
        put_slot(source, capacity + k, before[k].astype(f32))
        put_slot(source, capacity + EDGE + k, after[k].astype(f32))
    put_slot(source, capacity + 2 * EDGE, jnp.zeros((128, 256), f32))
    marked, stage = marked.ready(), own.ready()

    def own_slot(b, _):
        values = stage[b].astype(f32)
        put_slot(source, b, jnp.where(marked[b].astype(f32) < MARK_LIMIT, values, 0.0))
        return 0

    lax.fori_loop(0, capacity, own_slot, 0)
    indexing.ready()
    fetch.wait()

    def finish(b, total, carry):
        grad[b] = total
        return carry

    conv(index, source, windows, weights, True, capacity, finish, 0)


def first_conv_kernel(
    index_hbm, counts_hbm, rows, marked_hbm, before, after, vectors, weights_hbm,
    hidden_hbm, hidden, row, up, down, stats, source, windows, weights, sem, index, index_sem,
    marked_stage, marked_sem, counts, counts_sem, out_sem,
):
    capacity = hidden.shape[0]
    indexing = Fetched(index_hbm, index, index_sem)
    counting = Fetched(counts_hbm, counts, counts_sem)
    marked = Fetched(marked_hbm, marked_stage, marked_sem)
    fetch = pltpu.make_async_copy(weights_hbm, weights, sem)
    fetch.start()
    mean, inv_scale, voxel_total = combine_moments(rows[...])
    stats[...] = jnp.concatenate(
        [mean, inv_scale, voxel_total, jnp.zeros((5, 256), f32)], axis=0
    )
    slope = inv_scale * vectors[0:1, :]
    shift = vectors[1:2, :] - mean * slope

    def prepare(refs, k, slot):
        values = refs[0][k].astype(f32)
        pre = values * slope + shift
        put_slot(source, slot, jnp.where(values < MARK_LIMIT, pre * sigmoid(pre), 0.0))

    each_slot(capacity, (marked,), (before,), (after,), prepare)
    put_slot(source, capacity + 2 * EDGE, jnp.zeros((128, 256), f32))
    indexing.ready()
    fetch.wait()

    def kept(b):
        return pltpu.make_async_copy(hidden.at[b], hidden_hbm.at[b], out_sem.at[b])

    def finish(b, total, carry):
        on = marked_stage[b].astype(f32) < MARK_LIMIT
        rounded = total.astype(bf16).astype(f32)
        hidden[b] = jnp.where(on, rounded, MARK).astype(bf16)
        kept(b).start()
        return add_moments(carry, rounded, on, b == 0)

    moments = conv(index, source, windows, weights, False, capacity, finish, no_moments())
    live = counting.ready()[lax.axis_index(AXES)]
    for k in range(EDGE):
        up[k] = hidden[live - EDGE + k]
        down[k] = hidden[k]
    row[...] = jnp.broadcast_to(moments_row(moments), row.shape)
    for b in range(capacity):
        kept(b).wait()


def slope_of(pre):
    part = sigmoid(pre)
    return part * (1.0 + pre * (1.0 - part))


def second_sums_kernel(counts_hbm, rows, hidden, grad, vectors, row, stats, up, down, counts, counts_sem):
    counting = Fetched(counts_hbm, counts, counts_sem)
    capacity = hidden.shape[0]
    mean, inv_scale, voxel_total = combine_moments(rows[...])
    stats[...] = jnp.concatenate(
        [mean, inv_scale, voxel_total, jnp.zeros((5, 256), f32)], axis=0
    )
    gains, biases = vectors[2:3, :], vectors[3:4, :]

    def step(b, carry):
        values = hidden[b].astype(f32)
        normed = (values - mean) * inv_scale
        scaled = grad[b] * slope_of(normed * gains + biases) * gains
        on = values < MARK_LIMIT
        scaled = jnp.where(on, scaled, 0.0)
        normed = jnp.where(on, normed, 0.0)
        return carry[0] + eight_rows(scaled), carry[1] + eight_rows(scaled * normed)

    zero = jnp.zeros((8, 256), f32)
    first, second = lax.fori_loop(0, capacity, step, (zero, zero), unroll=2)
    live = counting.ready()[lax.axis_index(AXES)]
    for k in range(EDGE):
        up[k] = grad[live - EDGE + k].astype(bf16)
        down[k] = grad[k].astype(bf16)
    row[...] = jnp.broadcast_to(pairs_row(column_sum(first), column_sum(second)), row.shape)


def second_conv_kernel(
    index_hbm, hidden_hbm, before, after, stats, vectors, marked_hbm, weights_hbm,
    out, done, source, windows, weights, sem, index, index_sem, hidden_stage, hidden_sem, marked, marked_sem,
):
    capacity = marked.shape[0]
    indexing = Fetched(index_hbm, index, index_sem)
    hidden = Fetched(hidden_hbm, hidden_stage, hidden_sem)
    marking = Fetched(marked_hbm, marked, marked_sem)
    fetch = pltpu.make_async_copy(weights_hbm, weights, sem)
    fetch.start()
    done[...] = jnp.zeros(done.shape, f32)
    slope = stats[1:2, :] * vectors[2:3, :]
    shift = vectors[3:4, :] - stats[0:1, :] * slope

    def prepare(refs, k, slot):
        values = refs[0][k].astype(f32)
        pre = values * slope + shift
        put_slot(source, slot, jnp.where(values < MARK_LIMIT, pre * sigmoid(pre), 0.0))

    each_slot(capacity, (hidden,), (before,), (after,), prepare)
    put_slot(source, capacity + 2 * EDGE, jnp.zeros((128, 256), f32))
    marking.ready()
    indexing.ready()
    fetch.wait()

    def finish(b, total, carry):
        inputs = marked[b].astype(f32)
        out[b] = jnp.where(inputs < MARK_LIMIT, inputs + total, 0.0).astype(bf16)
        return carry

    conv(index, source, windows, weights, False, capacity, finish, 0)


def back_conv_kernel(
    index_hbm, rows, hidden_hbm, hid_before, hid_after, grad, grad_before, grad_after,
    stats_second, marked_hbm, stats_first, vectors, cotangent, weights_hbm, after_conv,
    partial, normed_out, row, source, windows, weights, sem, index, index_sem, hidden_stage, hidden_sem, marked, marked_sem,
    stage, stage_sem,
):
    capacity = marked.shape[0]
    indexing = Fetched(index_hbm, index, index_sem)
    hidden = Fetched(hidden_hbm, hidden_stage, hidden_sem)
    marking = Fetched(marked_hbm, marked, marked_sem)
    fetch = pltpu.make_async_copy(weights_hbm, weights, sem)
    fetch.start()
    own = Fetched(cotangent, stage, stage_sem)
    mean, inv_scale, voxel_total = (stats_second[k : k + 1, :] for k in range(3))
    first, second = combine_pairs(rows[...], voxel_total)
    gains, biases = vectors[2:3, :], vectors[3:4, :]

    def prepare(refs, k, slot):
        values = refs[0][k].astype(f32)
        normed = (values - mean) * inv_scale
        scaled = refs[1][k].astype(f32) * slope_of(normed * gains + biases) * gains
        result = inv_scale * (scaled - first - normed * second)
        put_slot(source, slot, jnp.where(values < MARK_LIMIT, result, 0.0))

    each_slot(capacity, (hidden, grad), (hid_before, grad_before), (hid_after, grad_after), prepare)
    put_slot(source, capacity + 2 * EDGE, jnp.zeros((128, 256), f32))
    marking.ready()
    indexing.ready()
    fetch.wait()
    own.ready()
    mean_first, inv_first = stats_first[0:1, :], stats_first[1:2, :]
    gains_first, biases_first = vectors[0:1, :], vectors[1:2, :]

    def finish(b, total, carry):
        values = marked[b].astype(f32)
        normed = (values - mean_first) * inv_first
        on = values < MARK_LIMIT
        scaled = total * slope_of(normed * gains_first + biases_first) * gains_first
        scaled = jnp.where(on, scaled, 0.0)
        normed = jnp.where(on, normed, 0.0)
        whole = stage[b].astype(f32) + inv_first * scaled
        partial[b] = jnp.where(on, whole, MARK)
        normed_out[b] = normed
        return carry[0] + eight_rows(scaled), carry[1] + eight_rows(scaled * normed)

    zero = jnp.zeros((8, 256), f32)
    sums = conv(index, source, windows, weights, True, capacity, finish, (zero, zero))
    row[...] = jnp.broadcast_to(pairs_row(column_sum(sums[0]), column_sum(sums[1])), row.shape)


def end_kernel(rows, partial, normed, stats, out_hbm, out, sem):
    capacity = partial.shape[0]
    inv_scale, voxel_total = stats[1:2, :], stats[2:3, :]
    first, second = combine_pairs(rows[...], voxel_total)
    first, second = inv_scale * first, inv_scale * second

    def done(b):
        return pltpu.make_async_copy(out.at[b], out_hbm.at[b], sem.at[b])

    def step(b, carry):
        whole = partial[b]
        out[b] = jnp.where(whole < MARK_LIMIT, whole - first - normed[b] * second, 0.0).astype(bf16)
        done(b).start()
        return carry

    lax.fori_loop(0, capacity, step, 0)
    for b in range(capacity):
        done(b).wait()


def on_device(
    features, voxel_mask, counts, neighbors, w_first, w_second,
    gain_first, bias_first, gain_second, bias_second, cotangent,
):
    capacity, voxels, channels = features.shape
    devices = counts.shape[0]
    vectors = [v.reshape(1, channels) for v in (gain_first, bias_first, gain_second, bias_second)]
    gain_first, bias_first, gain_second, bias_second = vectors
    w_first = w_first.reshape(27, channels, channels)
    w_second = w_second.reshape(27, channels, channels)

    def shift_up(x):
        return lax.ppermute(x, AXES, [(i, (i + 1) % devices) for i in range(devices)])

    def shift_down(x):
        return lax.ppermute(x, AXES, [((i + 1) % devices, i) for i in range(devices)])

    def exchange(row):
        return lax.all_to_all(row, AXES, 0, 0, tiled=True)

    whole = ((capacity, voxels, channels), bf16)
    whole_wide = ((capacity, voxels, channels), f32)
    table = (neighbors.shape, jnp.int32)
    edge = ((EDGE, voxels, channels), bf16)
    packed = ((devices, 128), f32)
    vector = ((8, channels), f32)
    slots = capacity + 2 * EDGE + 1

    dma = pltpu.SemaphoreType.DMA
    marked, marked_near, feat_up, feat_down, cot_up, cot_down, vectors = call(
        mark_kernel, "mark", [hbm()] * 8, [(*whole, "hbm"), whole, edge, edge, edge, edge, vector],
        [
            pltpu.VMEM(*whole), pltpu.VMEM((2 * EDGE, voxels, channels), bf16), dma((2 * EDGE,)),
            pltpu.VMEM((capacity, voxels), jnp.int32),
            pltpu.VMEM((4, 1, channels), f32),
            dma((capacity,)), dma((5,)), pltpu.SMEM(counts.shape, jnp.int32), dma, dma((capacity,)),
        ],
    )(counts, features, voxel_mask, cotangent, gain_first, bias_first, gain_second, bias_second)
    cot_before, cot_after = shift_up(cot_up), shift_down(cot_down)
    feat_before, feat_after = shift_up(feat_up), shift_down(feat_down)
    row, index = call(
        first_sums_kernel, "first_sums", [hbm(), vmem(), hbm()], [packed, (*table, "hbm")],
        [
            pltpu.SMEM(counts.shape, jnp.int32), dma, pltpu.VMEM(*table), dma, pltpu.VMEM(*table), dma,
        ],
    )(counts, marked_near, neighbors)
    rows_first = exchange(row)

    (grad,) = call(
        grad_conv_kernel, "grad_conv", [hbm(), hbm(), hbm(), vmem(), vmem(), hbm()],
        [whole_wide], conv_scratch(slots, capacity) + [pltpu.VMEM(*whole), dma] * 2,
    )(index, cotangent, marked, cot_before, cot_after, w_second)

    hidden, hidden_near, row, hid_up, hid_down, stats_first = call(
        first_conv_kernel, "first_conv",
        [hbm(), hbm(), vmem(), hbm(), vmem(), vmem(), vmem(), hbm()],
        [(*whole, "hbm"), whole, packed, edge, edge, vector],
        conv_scratch(slots, capacity)
        + [
            pltpu.VMEM(*whole), dma, pltpu.SMEM(counts.shape, jnp.int32), dma, dma((capacity,)),
        ],
    )(index, counts, rows_first, marked, feat_before, feat_after, vectors, w_first)
    rows_second = exchange(row)
    hid_before, hid_after = shift_up(hid_up), shift_down(hid_down)

    row, stats_second, grad_up, grad_down = call(
        second_sums_kernel, "second_sums", [hbm()] + [vmem()] * 4, [packed, vector, edge, edge],
        [pltpu.SMEM(counts.shape, jnp.int32), dma],
    )(
        counts, rows_second, hidden_near, grad, vectors
    )
    grad_before, grad_after = shift_up(grad_up), shift_down(grad_down)
    rows_third = exchange(row)

    output, done = call(
        second_conv_kernel, "second_conv", [hbm(), hbm(), vmem(), vmem(), vmem(), vmem(), hbm(), hbm()],
        [whole, ((8, 128), f32)],
        conv_scratch(slots, capacity) + [pltpu.VMEM(*whole), dma, pltpu.VMEM(*whole), dma],
    )(index, hidden, hid_before, hid_after, stats_second, vectors, marked, w_second)

    partial, normed, row = call(
        back_conv_kernel, "back_conv", [hbm(), vmem(), hbm()] + [vmem()] * 6 + [hbm(), vmem(), vmem(), hbm(), hbm(), vmem()],
        [whole_wide, whole_wide, packed],
        conv_scratch(slots, capacity) + [pltpu.VMEM(*whole), dma] * 3,
    )(
        index, rows_third, hidden, hid_before, hid_after, grad, grad_before, grad_after,
        stats_second, marked, stats_first, vectors, cotangent, w_first, done,
    )
    rows_fourth = exchange(row)

    (grad_features,) = call(
        end_kernel, "end", [vmem()] * 4, [(*whole, "hbm")], [pltpu.VMEM(*whole), dma((capacity,))]
    )(rows_fourth, partial, normed, stats_first)
    return (output, grad_features)


def solution(mesh):
    split = P(AXES, None, None)
    placed = (split, P(AXES, None), P(), P(AXES, None), P(), P(), P(), P(), P(), P(), split)
    return jax.shard_map(
        on_device, mesh=mesh, in_specs=placed, out_specs=(split, split), check_vma=False
    )
```

```python
import functools

import jax
import jax.numpy as jnp
from jax import lax
from jax.experimental import pallas as pl
from jax.experimental.pallas import tpu as pltpu
from jax.sharding import PartitionSpec as P

GC = 8
EDGE = 3
AXES = ("region", "sub")
eps_norm = 1e-05
MARK = 2.0**100
MARK_LIMIT = 2.0**90
VMEM_LIMIT = 20 * 2**20
COSTS = {"second_sums": 50, "second_conv": 8, "first_conv": 8}
f32 = jnp.float32
bf16 = jnp.bfloat16


def vmem():
    return pl.BlockSpec(memory_space=pltpu.VMEM)


def hbm():
    return pl.BlockSpec(memory_space=pltpu.HBM)


def call(kernel, name, in_specs, outs, scratch=()):
    made = pl.pallas_call(
        kernel,
        name=name,
        in_specs=in_specs,
        out_specs=[hbm() if len(o) == 3 else vmem() for o in outs],
        out_shape=[pltpu.HBM(*o[:2]) if len(o) == 3 else jax.ShapeDtypeStruct(*o) for o in outs],
        scratch_shapes=list(scratch),
        cost_estimate=pl.CostEstimate(flops=int(COSTS[name] * 1.15e9), bytes_accessed=0, transcendentals=0)
        if name in COSTS
        else None,
        compiler_params=pltpu.CompilerParams(vmem_limit_bytes=VMEM_LIMIT),
    )

    def run(*operands):
        return made(
            *(
                pltpu.with_memory_space_constraint(x, pltpu.HBM)
                if spec.memory_space == pltpu.HBM
                else x
                for spec, x in zip(in_specs, operands)
            )
        )

    return run


class Fetched:
    def __init__(self, source, target, sem):
        self.copy = pltpu.make_async_copy(source, target, sem)
        self.copy.start()
        self.target = target

    def ready(self):
        self.copy.wait()
        return self.target


def lane_of(shape):
    return lax.broadcasted_iota(jnp.int32, shape, len(shape) - 1) % GC


def spread_first(x):
    x = jnp.where(lane_of(x.shape) == 0, x, 0.0)
    for s in (1, 2, 4):
        x = x + pltpu.roll(x, s, 1)
    return x


def group_total(x):
    for s in (1, 2, 4):
        x = x + pltpu.roll(x, 128 - s, 1)
    return spread_first(x)


def halves(x):
    return x[:, :128], x[:, 128:]


def pack_row(values):
    lane = lane_of((1, 128))
    row = jnp.zeros((1, 128), f32)
    for k, value in enumerate(values):
        row = jnp.where(lane == k, value, row)
    return row


def unpack_row(rows, k):
    return spread_first(pltpu.roll(rows, 128 - k, 1) if k else rows)


def join(pair):
    return jnp.concatenate(pair, axis=1)


def column_sum(x):
    return jnp.sum(x, axis=0, keepdims=True)


def no_moments():
    zero = jnp.zeros((8, 256), f32)
    return zero, zero, zero, zero[:, :128]


def add_moments(moments, values, on, first):
    base, sums, squares, count = moments
    here = eight_rows(jnp.where(on[:, :128], 1.0, 0.0))
    number = jnp.maximum(here, 1.0)
    base = jnp.where(first, eight_rows(jnp.where(on, values, 0.0)) / join([number, number]), base)
    apart = jnp.where(on.reshape(16, 8, 256), values.reshape(16, 8, 256) - base, 0.0)
    sums = sums + jnp.sum(apart, axis=0)
    squares = squares + jnp.sum(apart * apart, axis=0)
    return base, sums, squares, count + here


def moments_row(moments):
    base, total, square, count = moments
    safe = jnp.maximum(count, 1.0)
    number = column_sum(count)
    sums, squares = [], []
    for base, total, square in zip(halves(base), halves(total), halves(square)):
        apart = total / safe
        mean = base + apart
        group_sum = group_total(column_sum(count * mean))
        group_mean = group_sum / jnp.maximum(number * float(GC), 1.0)
        about = square - total * apart + count * ((mean - group_mean) * (mean - group_mean))
        sums.append(group_sum)
        squares.append(group_total(column_sum(about)))
    return pack_row([*sums, *squares, number * float(GC)])


def combine_moments(rows):
    count = unpack_row(rows, 4)
    total = column_sum(count)
    safe = jnp.maximum(count, 1.0)
    means, scales = [], []
    for k in (0, 1):
        sums = unpack_row(rows, k)
        mean = column_sum(sums) / total
        apart = sums / safe - mean
        spread = column_sum(unpack_row(rows, 2 + k) + count * (apart * apart)) / total
        means.append(mean)
        scales.append(lax.rsqrt(spread + eps_norm))
    return join(means), join(scales), join([total, total])


def combine_pairs(rows, total):
    summed = column_sum(rows)
    first = join([unpack_row(summed, 0), unpack_row(summed, 1)]) / total
    second = join([unpack_row(summed, 2), unpack_row(summed, 3)]) / total
    return first, second


def pairs_row(first, second):
    return pack_row([group_total(h) for h in (*halves(first), *halves(second))])


def eight_rows(x):
    return jnp.sum(x.reshape(16, 8, x.shape[-1]), axis=0)


def put_slot(source, slot, values):
    tile = values.reshape(16, 8, 256)
    source[1, slot] = tile
    source[0, slot] = pltpu.roll(tile, 1, 1)
    source[2, slot] = pltpu.roll(tile, 7, 1)


def build(index, brick, source, windows):
    z = lax.broadcasted_iota(jnp.int32, (1, 8, 256), 1)
    for slab in range(6):
        dx, x = (0, 3) if slab == 0 else (2, 0) if slab == 5 else (1, slab - 1)
        for l in range(3):
            parts = []
            for dy, y, n in ((0, 3, 1), (1, 0, 4), (2, 0, 1)):
                at = pl.ds(x * 4 + y, n)
                part = source[l, index[brick, dx * 9 + dy * 3 + 1], at]
                if l != 1:
                    edge = source[l, index[brick, dx * 9 + dy * 3 + l], at]
                    part = jnp.where(z == (0 if l == 0 else 7), edge, part)
                parts.append(part)
            columns = jnp.concatenate(parts, axis=0)
            for j in range(3):
                windows[j * 3 + l, slab * 32 : slab * 32 + 32, :] = (
                    columns[j : j + 4].reshape(32, 256).astype(bf16)
                )


def product(pair, weights, backward):
    total = None
    for i in range(3):
        for j in range(3):
            for l in range(3):
                o = i * 9 + j * 3 + l
                taken = jnp.concatenate(
                    [pair[k, j * 3 + l, i * 32 : i * 32 + 128, :] for k in range(2)], axis=0
                )
                if backward:
                    part = lax.dot_general(
                        taken, weights[26 - o], (((1,), (1,)), ((), ())), preferred_element_type=f32
                    )
                else:
                    part = jnp.dot(taken, weights[o], preferred_element_type=f32)
                total = part if total is None else total + part
    return total


def conv(index, source, pairs, weights, backward, capacity, finish, carry):
    even, odd = pairs

    def build_pair(first, pair):
        first = jnp.minimum(first, capacity - 2)
        for k in range(2):
            build(index, first + k, source, pair.at[k])

    def finish_pair(first, pair, carry):
        both = product(pair, weights, backward)
        carry = finish(first, both[:128], carry)
        return finish(first + 1, both[128:], carry)

    build_pair(0, even)

    def four(step, carry):
        first = 4 * step
        build_pair(first + 2, odd)
        carry = finish_pair(first, even, carry)
        build_pair(first + 4, even)
        return finish_pair(first + 2, odd, carry)

    return lax.fori_loop(0, capacity // 4, four, carry)


def conv_scratch(slots, capacity):
    return [
        pltpu.VMEM((3, slots, 16, 8, 256), f32),
        pltpu.VMEM((2, 9, 192, 256), bf16),
        pltpu.VMEM((2, 9, 192, 256), bf16),
        pltpu.VMEM((27, 256, 256), bf16),
        pltpu.SemaphoreType.DMA,
        pltpu.SMEM((capacity, 27), jnp.int32),
        pltpu.SemaphoreType.DMA,
    ]


def each_slot(capacity, own, before, after, body):
    def run(refs, start, count):
        def step(k, _):
            body(refs, k, start + k)
            return 0

        lax.fori_loop(0, count, step, 0)

    run(before, capacity, EDGE)
    run(after, capacity + EDGE, EDGE)
    run([x.ready() if isinstance(x, Fetched) else x for x in own], 0, capacity)


def sigmoid(x):
    return 1.0 / (1.0 + jnp.exp(-x))


def mark_kernel(
    counts_hbm, features, mask, cotangent, gain_first, bias_first, gain_second, bias_second,
    marked, feat_up, feat_down, cot_up, cot_down, vectors,
    stage, cot_stage, cot_sem, mask_stage, vector_stage, feature_sem, small_sem, counts, counts_sem,
):
    capacity = marked.shape[0]
    counting = Fetched(counts_hbm, counts, counts_sem)
    small = [pltpu.make_async_copy(mask, mask_stage, small_sem.at[0])]
    for k, vector in enumerate((gain_first, bias_first, gain_second, bias_second)):
        small.append(pltpu.make_async_copy(vector, vector_stage.at[k], small_sem.at[k + 1]))

    def arriving(b):
        return pltpu.make_async_copy(features.at[b], stage.at[b], feature_sem.at[b])

    for copy in small + [arriving(b) for b in range(capacity)]:
        copy.start()
    live = counting.ready()[lax.axis_index(AXES)]
    edges = []
    for k in range(EDGE):
        for at, brick in ((k, live - EDGE + k), (EDGE + k, k)):
            edges.append(pltpu.make_async_copy(cotangent.at[brick], cot_stage.at[at], cot_sem.at[at]))
    for copy in edges:
        copy.start()
    small[0].wait()
    def step(b, _):
        wide = jnp.broadcast_to(mask_stage[pl.ds(b, 1), :].astype(f32), (128, 128)).T
        wide = wide * jnp.where(b < live, 1.0, 0.0)
        arriving(b).wait()
        marked[b] = jnp.where(join([wide, wide]) > 0.5, stage[b].astype(f32), MARK).astype(bf16)
        return 0

    lax.fori_loop(0, capacity, step, 0, unroll=4)
    for copy in edges:
        copy.wait()
    for k in range(EDGE):
        for feat, cot, at, brick in (
            (feat_up, cot_up, k, live - EDGE + k), (feat_down, cot_down, EDGE + k, k)
        ):
            values = marked[brick]
            feat[k] = values
            on = values.astype(f32) < MARK_LIMIT
            cot[k] = jnp.where(on, cot_stage[at].astype(f32), 0.0).astype(bf16)
    for copy in small[1:]:
        copy.wait()
    for k in range(4):
        vectors[k : k + 1, :] = vector_stage[k]
    vectors[4:8, :] = jnp.zeros((4, 256), f32)


def first_sums_kernel(
    counts_hbm, marked, neighbors_hbm, row, index_hbm, marked_hbm, out_sem,
    counts, counts_sem, neighbors, neighbors_sem, index, index_sem,
):
    counting = Fetched(counts_hbm, counts, counts_sem)
    naming = Fetched(neighbors_hbm, neighbors, neighbors_sem)
    kept = pltpu.make_async_copy(marked, marked_hbm, out_sem)
    kept.start()
    device = lax.axis_index(AXES)
    counting.ready()

    capacity = marked.shape[0]
    live_before = counts[jnp.maximum(device - 1, 0)]
    named = naming.ready()[...]
    owner = lax.div(named, capacity)
    within = named - owner * capacity
    slot = jnp.where(
        owner == device,
        within,
        jnp.where(
            owner == device - 1, within + (capacity + EDGE - live_before), within + (capacity + EDGE)
        ),
    )
    index[...] = jnp.where(named < 0, capacity + 2 * EDGE, slot)
    indexed = pltpu.make_async_copy(index, index_hbm, index_sem)
    indexed.start()


    def step(b, moments):
        values = marked[b].astype(f32)
        return add_moments(moments, values, values < MARK_LIMIT, b == 0)

    moments = lax.fori_loop(0, capacity, step, no_moments(), unroll=2)
    row[...] = jnp.broadcast_to(moments_row(moments), row.shape)
    indexed.wait()
    kept.wait()


def grad_conv_kernel(
    index_hbm, cotangent, marked_hbm, before, after, weights_hbm,
    grad, source, even, odd, weights, sem, index, index_sem, stage, stage_sem, marked, marked_sem,
):
    capacity = marked.shape[0]
    indexing = Fetched(index_hbm, index, index_sem)
    own = Fetched(cotangent, stage, stage_sem)
    marked = Fetched(marked_hbm, marked, marked_sem)
    fetch = pltpu.make_async_copy(weights_hbm, weights, sem)
    fetch.start()
    for k in range(EDGE):
        put_slot(source, capacity + k, before[k].astype(f32))
        put_slot(source, capacity + EDGE + k, after[k].astype(f32))
    put_slot(source, capacity + 2 * EDGE, jnp.zeros((128, 256), f32))
    marked, stage = marked.ready(), own.ready()

    def own_slot(b, _):
        values = stage[b].astype(f32)
        put_slot(source, b, jnp.where(marked[b].astype(f32) < MARK_LIMIT, values, 0.0))
        return 0

    lax.fori_loop(0, capacity, own_slot, 0)
    indexing.ready()
    fetch.wait()

    def finish(b, total, carry):
        grad[b] = total
        return carry

    conv(index, source, (even, odd), weights, True, capacity, finish, 0)


def first_conv_kernel(
    index_hbm, counts_hbm, rows, marked_hbm, before, after, vectors, weights_hbm,
    hidden, row, up, down, stats, source, even, odd, weights, sem, index, index_sem,
    marked_stage, marked_sem, counts, counts_sem,
):
    capacity = hidden.shape[0]
    indexing = Fetched(index_hbm, index, index_sem)
    counting = Fetched(counts_hbm, counts, counts_sem)
    marked = Fetched(marked_hbm, marked_stage, marked_sem)
    fetch = pltpu.make_async_copy(weights_hbm, weights, sem)
    fetch.start()
    mean, inv_scale, voxel_total = combine_moments(rows[...])
    stats[...] = jnp.concatenate(
        [mean, inv_scale, voxel_total, jnp.zeros((5, 256), f32)], axis=0
    )
    slope = inv_scale * vectors[0:1, :]
    shift = vectors[1:2, :] - mean * slope

    def prepare(refs, k, slot):
        values = refs[0][k].astype(f32)
        pre = values * slope + shift
        put_slot(source, slot, jnp.where(values < MARK_LIMIT, pre * sigmoid(pre), 0.0))

    each_slot(capacity, (marked,), (before,), (after,), prepare)
    put_slot(source, capacity + 2 * EDGE, jnp.zeros((128, 256), f32))
    indexing.ready()
    fetch.wait()

    def finish(b, total, carry):
        on = marked_stage[b].astype(f32) < MARK_LIMIT
        rounded = total.astype(bf16).astype(f32)
        hidden[b] = jnp.where(on, rounded, MARK).astype(bf16)
        return add_moments(carry, rounded, on, b == 0)

    moments = conv(index, source, (even, odd), weights, False, capacity, finish, no_moments())
    live = counting.ready()[lax.axis_index(AXES)]
    for k in range(EDGE):
        up[k] = hidden[live - EDGE + k]
        down[k] = hidden[k]
    row[...] = jnp.broadcast_to(moments_row(moments), row.shape)


def slope_of(pre):
    part = sigmoid(pre)
    return part * (1.0 + pre * (1.0 - part))


def second_sums_kernel(counts_hbm, rows, hidden, grad, vectors, row, stats, up, down, hidden_hbm, counts, counts_sem, out_sem):
    counting = Fetched(counts_hbm, counts, counts_sem)
    kept = pltpu.make_async_copy(hidden, hidden_hbm, out_sem)
    kept.start()
    capacity = hidden.shape[0]
    mean, inv_scale, voxel_total = combine_moments(rows[...])
    stats[...] = jnp.concatenate(
        [mean, inv_scale, voxel_total, jnp.zeros((5, 256), f32)], axis=0
    )
    gains, biases = vectors[2:3, :], vectors[3:4, :]

    def step(b, carry):
        values = hidden[b].astype(f32)
        normed = (values - mean) * inv_scale
        scaled = grad[b] * slope_of(normed * gains + biases) * gains
        on = values < MARK_LIMIT
        scaled = jnp.where(on, scaled, 0.0)
        normed = jnp.where(on, normed, 0.0)
        return carry[0] + eight_rows(scaled), carry[1] + eight_rows(scaled * normed)

    zero = jnp.zeros((8, 256), f32)
    first, second = lax.fori_loop(0, capacity, step, (zero, zero), unroll=2)
    live = counting.ready()[lax.axis_index(AXES)]
    for k in range(EDGE):
        up[k] = grad[live - EDGE + k].astype(bf16)
        down[k] = grad[k].astype(bf16)
    kept.wait()
    row[...] = jnp.broadcast_to(pairs_row(column_sum(first), column_sum(second)), row.shape)


def second_conv_kernel(
    index_hbm, hidden_hbm, before, after, stats, vectors, marked_hbm, weights_hbm,
    out, done, source, even, odd, weights, sem, index, index_sem, hidden_stage, hidden_sem, marked, marked_sem,
):
    capacity = marked.shape[0]
    indexing = Fetched(index_hbm, index, index_sem)
    hidden = Fetched(hidden_hbm, hidden_stage, hidden_sem)
    marking = Fetched(marked_hbm, marked, marked_sem)
    fetch = pltpu.make_async_copy(weights_hbm, weights, sem)
    fetch.start()
    done[...] = jnp.zeros(done.shape, f32)
    slope = stats[1:2, :] * vectors[2:3, :]
    shift = vectors[3:4, :] - stats[0:1, :] * slope

    def prepare(refs, k, slot):
        values = refs[0][k].astype(f32)
        pre = values * slope + shift
        put_slot(source, slot, jnp.where(values < MARK_LIMIT, pre * sigmoid(pre), 0.0))

    each_slot(capacity, (hidden,), (before,), (after,), prepare)
    put_slot(source, capacity + 2 * EDGE, jnp.zeros((128, 256), f32))
    marking.ready()
    indexing.ready()
    fetch.wait()

    def finish(b, total, carry):
        inputs = marked[b].astype(f32)
        out[b] = jnp.where(inputs < MARK_LIMIT, inputs + total, 0.0).astype(bf16)
        return carry

    conv(index, source, (even, odd), weights, False, capacity, finish, 0)


def back_conv_kernel(
    index_hbm, rows, hidden_hbm, hid_before, hid_after, grad, grad_before, grad_after,
    stats_second, marked_hbm, stats_first, vectors, cotangent, weights_hbm, after_conv,
    partial, normed_out, row, source, even, odd, weights, sem, index, index_sem, hidden_stage, hidden_sem, marked, marked_sem,
    stage, stage_sem,
):
    capacity = marked.shape[0]
    indexing = Fetched(index_hbm, index, index_sem)
    hidden = Fetched(hidden_hbm, hidden_stage, hidden_sem)
    marking = Fetched(marked_hbm, marked, marked_sem)
    fetch = pltpu.make_async_copy(weights_hbm, weights, sem)
    fetch.start()
    own = Fetched(cotangent, stage, stage_sem)
    mean, inv_scale, voxel_total = (stats_second[k : k + 1, :] for k in range(3))
    first, second = combine_pairs(rows[...], voxel_total)
    gains, biases = vectors[2:3, :], vectors[3:4, :]

    def prepare(refs, k, slot):
        values = refs[0][k].astype(f32)
        normed = (values - mean) * inv_scale
        scaled = refs[1][k].astype(f32) * slope_of(normed * gains + biases) * gains
        result = inv_scale * (scaled - first - normed * second)
        put_slot(source, slot, jnp.where(values < MARK_LIMIT, result, 0.0))

    each_slot(capacity, (hidden, grad), (hid_before, grad_before), (hid_after, grad_after), prepare)
    put_slot(source, capacity + 2 * EDGE, jnp.zeros((128, 256), f32))
    marking.ready()
    indexing.ready()
    fetch.wait()
    own.ready()
    mean_first, inv_first = stats_first[0:1, :], stats_first[1:2, :]
    gains_first, biases_first = vectors[0:1, :], vectors[1:2, :]

    def finish(b, total, carry):
        values = marked[b].astype(f32)
        normed = (values - mean_first) * inv_first
        on = values < MARK_LIMIT
        scaled = total * slope_of(normed * gains_first + biases_first) * gains_first
        scaled = jnp.where(on, scaled, 0.0)
        normed = jnp.where(on, normed, 0.0)
        whole = stage[b].astype(f32) + inv_first * scaled
        partial[b] = jnp.where(on, whole, MARK)
        normed_out[b] = normed
        return carry[0] + eight_rows(scaled), carry[1] + eight_rows(scaled * normed)

    zero = jnp.zeros((8, 256), f32)
    sums = conv(index, source, (even, odd), weights, True, capacity, finish, (zero, zero))
    row[...] = jnp.broadcast_to(pairs_row(column_sum(sums[0]), column_sum(sums[1])), row.shape)


def end_kernel(rows, partial, normed, stats, out_hbm, out, sem):
    capacity = partial.shape[0]
    inv_scale, voxel_total = stats[1:2, :], stats[2:3, :]
    first, second = combine_pairs(rows[...], voxel_total)
    first, second = inv_scale * first, inv_scale * second

    def done(b):
        return pltpu.make_async_copy(out.at[b], out_hbm.at[b], sem.at[b])

    def step(b, carry):
        whole = partial[b]
        out[b] = jnp.where(whole < MARK_LIMIT, whole - first - normed[b] * second, 0.0).astype(bf16)
        done(b).start()
        return carry

    lax.fori_loop(0, capacity, step, 0)
    for b in range(capacity):
        done(b).wait()


def on_device(
    features, voxel_mask, counts, neighbors, w_first, w_second,
    gain_first, bias_first, gain_second, bias_second, cotangent,
):
    capacity, voxels, channels = features.shape
    devices = counts.shape[0]
    vectors = [v.reshape(1, channels) for v in (gain_first, bias_first, gain_second, bias_second)]
    gain_first, bias_first, gain_second, bias_second = vectors
    w_first = w_first.reshape(27, channels, channels)
    w_second = w_second.reshape(27, channels, channels)

    def shift_up(x):
        return lax.ppermute(x, AXES, [(i, (i + 1) % devices) for i in range(devices)])

    def shift_down(x):
        return lax.ppermute(x, AXES, [((i + 1) % devices, i) for i in range(devices)])

    def exchange(row):
        return lax.all_to_all(row, AXES, 0, 0, tiled=True)

    whole = ((capacity, voxels, channels), bf16)
    whole_wide = ((capacity, voxels, channels), f32)
    table = (neighbors.shape, jnp.int32)
    edge = ((EDGE, voxels, channels), bf16)
    packed = ((devices, 128), f32)
    vector = ((8, channels), f32)
    slots = capacity + 2 * EDGE + 1

    dma = pltpu.SemaphoreType.DMA
    marked_near, feat_up, feat_down, cot_up, cot_down, vectors = call(
        mark_kernel, "mark", [hbm()] * 8, [whole, edge, edge, edge, edge, vector],
        [
            pltpu.VMEM(*whole), pltpu.VMEM((2 * EDGE, voxels, channels), bf16), dma((2 * EDGE,)),
            pltpu.VMEM((capacity, voxels), jnp.int32),
            pltpu.VMEM((4, 1, channels), f32),
            dma((capacity,)), dma((5,)), pltpu.SMEM(counts.shape, jnp.int32), dma,
        ],
    )(counts, features, voxel_mask, cotangent, gain_first, bias_first, gain_second, bias_second)
    cot_before, cot_after = shift_up(cot_up), shift_down(cot_down)
    feat_before, feat_after = shift_up(feat_up), shift_down(feat_down)
    row, index, marked = call(
        first_sums_kernel, "first_sums", [hbm(), vmem(), hbm()], [packed, (*table, "hbm"), (*whole, "hbm")],
        [
            dma,
            pltpu.SMEM(counts.shape, jnp.int32), dma, pltpu.VMEM(*table), dma, pltpu.VMEM(*table), dma,
        ],
    )(counts, marked_near, neighbors)
    rows_first = exchange(row)

    (grad,) = call(
        grad_conv_kernel, "grad_conv", [hbm(), hbm(), hbm(), vmem(), vmem(), hbm()],
        [whole_wide], conv_scratch(slots, capacity) + [pltpu.VMEM(*whole), dma] * 2,
    )(index, cotangent, marked, cot_before, cot_after, w_second)

    hidden_near, row, hid_up, hid_down, stats_first = call(
        first_conv_kernel, "first_conv",
        [hbm(), hbm(), vmem(), hbm(), vmem(), vmem(), vmem(), hbm()],
        [whole, packed, edge, edge, vector],
        conv_scratch(slots, capacity)
        + [
            pltpu.VMEM(*whole), dma, pltpu.SMEM(counts.shape, jnp.int32), dma,
        ],
    )(index, counts, rows_first, marked, feat_before, feat_after, vectors, w_first)
    rows_second = exchange(row)
    hid_before, hid_after = shift_up(hid_up), shift_down(hid_down)

    row, stats_second, grad_up, grad_down, hidden = call(
        second_sums_kernel, "second_sums", [hbm()] + [vmem()] * 4, [packed, vector, edge, edge, (*whole, "hbm")],
        [pltpu.SMEM(counts.shape, jnp.int32), dma, dma],
    )(
        counts, rows_second, hidden_near, grad, vectors
    )
    grad_before, grad_after = shift_up(grad_up), shift_down(grad_down)
    rows_third = exchange(row)

    output, done = call(
        second_conv_kernel, "second_conv", [hbm(), hbm(), vmem(), vmem(), vmem(), vmem(), hbm(), hbm()],
        [whole, ((8, 128), f32)],
        conv_scratch(slots, capacity) + [pltpu.VMEM(*whole), dma, pltpu.VMEM(*whole), dma],
    )(index, hidden, hid_before, hid_after, stats_second, vectors, marked, w_second)

    partial, normed, row = call(
        back_conv_kernel, "back_conv", [hbm(), vmem(), hbm()] + [vmem()] * 6 + [hbm(), vmem(), vmem(), hbm(), hbm(), vmem()],
        [whole_wide, whole_wide, packed],
        conv_scratch(slots, capacity) + [pltpu.VMEM(*whole), dma] * 3,
    )(
        index, rows_third, hidden, hid_before, hid_after, grad, grad_before, grad_after,
        stats_second, marked, stats_first, vectors, cotangent, w_first, done,
    )
    rows_fourth = exchange(row)

    (grad_features,) = call(
        end_kernel, "end", [vmem()] * 4, [(*whole, "hbm")], [pltpu.VMEM(*whole), dma((capacity,))]
    )(rows_fourth, partial, normed, stats_first)
    return (output, grad_features)


def solution(mesh):
    split = P(AXES, None, None)
    placed = (split, P(AXES, None), P(), P(AXES, None), P(), P(), P(), P(), P(), P(), split)
    return jax.shard_map(
        on_device, mesh=mesh, in_specs=placed, out_specs=(split, split), check_vma=False
    )
```

```python
import functools

import jax
import jax.numpy as jnp
from jax import lax
from jax.experimental import pallas as pl
from jax.experimental.pallas import tpu as pltpu
from jax.sharding import PartitionSpec as P

GC = 8
EDGE = 3
AXES = ("region", "sub")
eps_norm = 1e-05
MARK = 2.0**100
MARK_LIMIT = 2.0**90
VMEM_LIMIT = 20 * 2**20
COSTS = {"second_sums": 50, "second_conv": 8, "first_conv": 8}
f32 = jnp.float32
bf16 = jnp.bfloat16


def vmem():
    return pl.BlockSpec(memory_space=pltpu.VMEM)


def hbm():
    return pl.BlockSpec(memory_space=pltpu.HBM)


def call(kernel, name, in_specs, outs, scratch=()):
    made = pl.pallas_call(
        kernel,
        name=name,
        in_specs=in_specs,
        out_specs=[hbm() if len(o) == 3 else vmem() for o in outs],
        out_shape=[pltpu.HBM(*o[:2]) if len(o) == 3 else jax.ShapeDtypeStruct(*o) for o in outs],
        scratch_shapes=list(scratch),
        cost_estimate=pl.CostEstimate(flops=int(COSTS[name] * 1.15e9), bytes_accessed=0, transcendentals=0)
        if name in COSTS
        else None,
        compiler_params=pltpu.CompilerParams(vmem_limit_bytes=VMEM_LIMIT),
    )

    def run(*operands):
        return made(
            *(
                pltpu.with_memory_space_constraint(x, pltpu.HBM)
                if spec.memory_space == pltpu.HBM
                else x
                for spec, x in zip(in_specs, operands)
            )
        )

    return run


class Fetched:
    def __init__(self, source, target, sem):
        self.copy = pltpu.make_async_copy(source, target, sem)
        self.copy.start()
        self.target = target

    def ready(self):
        self.copy.wait()
        return self.target


def lane_of(shape):
    return lax.broadcasted_iota(jnp.int32, shape, len(shape) - 1) % GC


def spread_first(x):
    x = jnp.where(lane_of(x.shape) == 0, x, 0.0)
    for s in (1, 2, 4):
        x = x + pltpu.roll(x, s, 1)
    return x


def group_total(x):
    for s in (1, 2, 4):
        x = x + pltpu.roll(x, 128 - s, 1)
    return spread_first(x)


def halves(x):
    return x[:, :128], x[:, 128:]


def pack_row(values):
    lane = lane_of((1, 128))
    row = jnp.zeros((1, 128), f32)
    for k, value in enumerate(values):
        row = jnp.where(lane == k, value, row)
    return row


def unpack_row(rows, k):
    return spread_first(pltpu.roll(rows, 128 - k, 1) if k else rows)


def join(pair):
    return jnp.concatenate(pair, axis=1)


def column_sum(x):
    return jnp.sum(x, axis=0, keepdims=True)


def no_moments():
    zero = jnp.zeros((8, 256), f32)
    return zero, zero, zero, zero[:, :128]


def add_moments(moments, values, on, first):
    base, sums, squares, count = moments
    here = eight_rows(jnp.where(on[:, :128], 1.0, 0.0))
    number = jnp.maximum(here, 1.0)
    base = jnp.where(first, eight_rows(jnp.where(on, values, 0.0)) / join([number, number]), base)
    apart = jnp.where(on.reshape(16, 8, 256), values.reshape(16, 8, 256) - base, 0.0)
    sums = sums + jnp.sum(apart, axis=0)
    squares = squares + jnp.sum(apart * apart, axis=0)
    return base, sums, squares, count + here


def moments_row(moments):
    base, total, square, count = moments
    safe = jnp.maximum(count, 1.0)
    number = column_sum(count)
    sums, squares = [], []
    for base, total, square in zip(halves(base), halves(total), halves(square)):
        apart = total / safe
        mean = base + apart
        group_sum = group_total(column_sum(count * mean))
        group_mean = group_sum / jnp.maximum(number * float(GC), 1.0)
        about = square - total * apart + count * ((mean - group_mean) * (mean - group_mean))
        sums.append(group_sum)
        squares.append(group_total(column_sum(about)))
    return pack_row([*sums, *squares, number * float(GC)])


def combine_moments(rows):
    count = unpack_row(rows, 4)
    total = column_sum(count)
    safe = jnp.maximum(count, 1.0)
    means, scales = [], []
    for k in (0, 1):
        sums = unpack_row(rows, k)
        mean = column_sum(sums) / total
        apart = sums / safe - mean
        spread = column_sum(unpack_row(rows, 2 + k) + count * (apart * apart)) / total
        means.append(mean)
        scales.append(lax.rsqrt(spread + eps_norm))
    return join(means), join(scales), join([total, total])


def combine_pairs(rows, total):
    summed = column_sum(rows)
    first = join([unpack_row(summed, 0), unpack_row(summed, 1)]) / total
    second = join([unpack_row(summed, 2), unpack_row(summed, 3)]) / total
    return first, second


def pairs_row(first, second):
    return pack_row([group_total(h) for h in (*halves(first), *halves(second))])


def eight_rows(x):
    return jnp.sum(x.reshape(16, 8, x.shape[-1]), axis=0)


def put_slot(source, slot, values):
    tile = values.reshape(16, 8, 256)
    source[1, slot] = tile
    source[0, slot] = pltpu.roll(tile, 1, 1)
    source[2, slot] = pltpu.roll(tile, 7, 1)


def build(index, brick, source, windows):
    z = lax.broadcasted_iota(jnp.int32, (1, 8, 256), 1)
    for slab in range(6):
        dx, x = (0, 3) if slab == 0 else (2, 0) if slab == 5 else (1, slab - 1)
        for l in range(3):
            parts = []
            for dy, y, n in ((0, 3, 1), (1, 0, 4), (2, 0, 1)):
                at = pl.ds(x * 4 + y, n)
                part = source[l, index[brick, dx * 9 + dy * 3 + 1], at]
                if l != 1:
                    edge = source[l, index[brick, dx * 9 + dy * 3 + l], at]
                    part = jnp.where(z == (0 if l == 0 else 7), edge, part)
                parts.append(part)
            columns = jnp.concatenate(parts, axis=0)
            for j in range(3):
                windows[j * 3 + l, slab * 32 : slab * 32 + 32, :] = (
                    columns[j : j + 4].reshape(32, 256).astype(bf16)
                )


def product(pair, weights, backward):
    total = None
    for i in range(3):
        for j in range(3):
            for l in range(3):
                o = i * 9 + j * 3 + l
                taken = jnp.concatenate(
                    [pair[k, j * 3 + l, i * 32 : i * 32 + 128, :] for k in range(2)], axis=0
                )
                if backward:
                    part = lax.dot_general(
                        taken, weights[26 - o], (((1,), (1,)), ((), ())), preferred_element_type=f32
                    )
                else:
                    part = jnp.dot(taken, weights[o], preferred_element_type=f32)
                total = part if total is None else total + part
    return total


def conv(index, source, pairs, weights, backward, capacity, finish, carry):
    even, odd = pairs

    def build_pair(first, pair):
        first = jnp.minimum(first, capacity - 2)
        for k in range(2):
            build(index, first + k, source, pair.at[k])

    def finish_pair(first, pair, carry):
        both = product(pair, weights, backward)
        carry = finish(first, both[:128], carry)
        return finish(first + 1, both[128:], carry)

    build_pair(0, even)

    def four(step, carry):
        first = 4 * step
        build_pair(first + 2, odd)
        carry = finish_pair(first, even, carry)
        build_pair(first + 4, even)
        return finish_pair(first + 2, odd, carry)

    return lax.fori_loop(0, capacity // 4, four, carry)


def conv_scratch(slots, capacity):
    return [
        pltpu.VMEM((3, slots, 16, 8, 256), f32),
        pltpu.VMEM((2, 9, 192, 256), bf16),
        pltpu.VMEM((2, 9, 192, 256), bf16),
        pltpu.VMEM((27, 256, 256), bf16),
        pltpu.SemaphoreType.DMA,
        pltpu.SMEM((capacity, 27), jnp.int32),
        pltpu.SemaphoreType.DMA,
    ]


def each_slot(capacity, own, before, after, body):
    def run(refs, start, count):
        def step(k, _):
            body(refs, k, start + k)
            return 0

        lax.fori_loop(0, count, step, 0)

    run(before, capacity, EDGE)
    run(after, capacity + EDGE, EDGE)
    run([x.ready() if isinstance(x, Fetched) else x for x in own], 0, capacity)


def sigmoid(x):
    return 1.0 / (1.0 + jnp.exp(-x))


def mark_kernel(
    counts_hbm, neighbors_hbm, features, mask, cotangent, gain_first, bias_first, gain_second, bias_second,
    marked, feat_up, feat_down, cot_up, cot_down, vectors, index_hbm,
    neighbors, neighbors_sem, index, index_sem,
    stage, cot_stage, cot_sem, mask_stage, vector_stage, feature_sem, small_sem, counts, counts_sem,
):
    capacity = marked.shape[0]
    counting = Fetched(counts_hbm, counts, counts_sem)
    naming = Fetched(neighbors_hbm, neighbors, neighbors_sem)
    small = [pltpu.make_async_copy(mask, mask_stage, small_sem.at[0])]
    for k, vector in enumerate((gain_first, bias_first, gain_second, bias_second)):
        small.append(pltpu.make_async_copy(vector, vector_stage.at[k], small_sem.at[k + 1]))

    def arriving(b):
        return pltpu.make_async_copy(features.at[b], stage.at[b], feature_sem.at[b])

    for copy in small + [arriving(b) for b in range(capacity)]:
        copy.start()
    device = lax.axis_index(AXES)
    live = counting.ready()[device]
    edges = []
    for k in range(EDGE):
        for at, brick in ((k, live - EDGE + k), (EDGE + k, k)):
            edges.append(pltpu.make_async_copy(cotangent.at[brick], cot_stage.at[at], cot_sem.at[at]))
    for copy in edges:
        copy.start()

    live_before = counts[jnp.maximum(device - 1, 0)]
    named = naming.ready()[...]
    owner = lax.div(named, capacity)
    within = named - owner * capacity
    slot = jnp.where(
        owner == device,
        within,
        jnp.where(
            owner == device - 1, within + (capacity + EDGE - live_before), within + (capacity + EDGE)
        ),
    )
    index[...] = jnp.where(named < 0, capacity + 2 * EDGE, slot)
    indexed = pltpu.make_async_copy(index, index_hbm, index_sem)
    indexed.start()

    small[0].wait()
    def step(b, _):
        wide = jnp.broadcast_to(mask_stage[pl.ds(b, 1), :].astype(f32), (128, 128)).T
        wide = wide * jnp.where(b < live, 1.0, 0.0)
        arriving(b).wait()
        marked[b] = jnp.where(join([wide, wide]) > 0.5, stage[b].astype(f32), MARK).astype(bf16)
        return 0

    lax.fori_loop(0, capacity, step, 0, unroll=4)
    for copy in edges:
        copy.wait()
    for k in range(EDGE):
        for feat, cot, at, brick in (
            (feat_up, cot_up, k, live - EDGE + k), (feat_down, cot_down, EDGE + k, k)
        ):
            values = marked[brick]
            feat[k] = values
            on = values.astype(f32) < MARK_LIMIT
            cot[k] = jnp.where(on, cot_stage[at].astype(f32), 0.0).astype(bf16)
    indexed.wait()
    for copy in small[1:]:
        copy.wait()
    for k in range(4):
        vectors[k : k + 1, :] = vector_stage[k]
    vectors[4:8, :] = jnp.zeros((4, 256), f32)


def first_sums_kernel(marked, row, marked_hbm, out_sem):
    kept = pltpu.make_async_copy(marked, marked_hbm, out_sem)
    kept.start()
    capacity = marked.shape[0]


    def step(b, moments):
        values = marked[b].astype(f32)
        return add_moments(moments, values, values < MARK_LIMIT, b == 0)

    moments = lax.fori_loop(0, capacity, step, no_moments(), unroll=4)
    row[...] = jnp.broadcast_to(moments_row(moments), row.shape)
    kept.wait()


def grad_conv_kernel(
    index_hbm, cotangent, marked_hbm, before, after, weights_hbm,
    grad, source, even, odd, weights, sem, index, index_sem, stage, stage_sem, marked, marked_sem,
):
    capacity = marked.shape[0]
    indexing = Fetched(index_hbm, index, index_sem)
    own = Fetched(cotangent, stage, stage_sem)
    marked = Fetched(marked_hbm, marked, marked_sem)
    fetch = pltpu.make_async_copy(weights_hbm, weights, sem)
    fetch.start()
    for k in range(EDGE):
        put_slot(source, capacity + k, before[k].astype(f32))
        put_slot(source, capacity + EDGE + k, after[k].astype(f32))
    put_slot(source, capacity + 2 * EDGE, jnp.zeros((128, 256), f32))
    marked, stage = marked.ready(), own.ready()

    def own_slot(b, _):
        values = stage[b].astype(f32)
        put_slot(source, b, jnp.where(marked[b].astype(f32) < MARK_LIMIT, values, 0.0))
        return 0

    lax.fori_loop(0, capacity, own_slot, 0)
    indexing.ready()
    fetch.wait()

    def finish(b, total, carry):
        grad[b] = total
        return carry

    conv(index, source, (even, odd), weights, True, capacity, finish, 0)


def first_conv_kernel(
    index_hbm, counts_hbm, rows, marked_hbm, before, after, vectors, weights_hbm,
    hidden, row, up, down, stats, source, even, odd, weights, sem, index, index_sem,
    marked_stage, marked_sem, counts, counts_sem,
):
    capacity = hidden.shape[0]
    indexing = Fetched(index_hbm, index, index_sem)
    counting = Fetched(counts_hbm, counts, counts_sem)
    marked = Fetched(marked_hbm, marked_stage, marked_sem)
    fetch = pltpu.make_async_copy(weights_hbm, weights, sem)
    fetch.start()
    mean, inv_scale, voxel_total = combine_moments(rows[...])
    stats[...] = jnp.concatenate(
        [mean, inv_scale, voxel_total, jnp.zeros((5, 256), f32)], axis=0
    )
    slope = inv_scale * vectors[0:1, :]
    shift = vectors[1:2, :] - mean * slope

    def prepare(refs, k, slot):
        values = refs[0][k].astype(f32)
        pre = values * slope + shift
        put_slot(source, slot, jnp.where(values < MARK_LIMIT, pre * sigmoid(pre), 0.0))

    each_slot(capacity, (marked,), (before,), (after,), prepare)
    put_slot(source, capacity + 2 * EDGE, jnp.zeros((128, 256), f32))
    indexing.ready()
    fetch.wait()

    def finish(b, total, carry):
        on = marked_stage[b].astype(f32) < MARK_LIMIT
        rounded = total.astype(bf16).astype(f32)
        hidden[b] = jnp.where(on, rounded, MARK).astype(bf16)
        return add_moments(carry, rounded, on, b == 0)

    moments = conv(index, source, (even, odd), weights, False, capacity, finish, no_moments())
    live = counting.ready()[lax.axis_index(AXES)]
    for k in range(EDGE):
        up[k] = hidden[live - EDGE + k]
        down[k] = hidden[k]
    row[...] = jnp.broadcast_to(moments_row(moments), row.shape)


def slope_of(pre):
    part = sigmoid(pre)
    return part * (1.0 + pre * (1.0 - part))


def second_sums_kernel(counts_hbm, rows, hidden, grad, vectors, row, stats, up, down, hidden_hbm, counts, counts_sem, out_sem):
    counting = Fetched(counts_hbm, counts, counts_sem)
    kept = pltpu.make_async_copy(hidden, hidden_hbm, out_sem)
    kept.start()
    capacity = hidden.shape[0]
    mean, inv_scale, voxel_total = combine_moments(rows[...])
    stats[...] = jnp.concatenate(
        [mean, inv_scale, voxel_total, jnp.zeros((5, 256), f32)], axis=0
    )
    gains, biases = vectors[2:3, :], vectors[3:4, :]

    def step(b, carry):
        values = hidden[b].astype(f32)
        normed = (values - mean) * inv_scale
        scaled = grad[b] * slope_of(normed * gains + biases) * gains
        on = values < MARK_LIMIT
        scaled = jnp.where(on, scaled, 0.0)
        normed = jnp.where(on, normed, 0.0)
        return carry[0] + eight_rows(scaled), carry[1] + eight_rows(scaled * normed)

    zero = jnp.zeros((8, 256), f32)
    first, second = lax.fori_loop(0, capacity, step, (zero, zero), unroll=2)
    live = counting.ready()[lax.axis_index(AXES)]
    for k in range(EDGE):
        up[k] = grad[live - EDGE + k].astype(bf16)
        down[k] = grad[k].astype(bf16)
    kept.wait()
    row[...] = jnp.broadcast_to(pairs_row(column_sum(first), column_sum(second)), row.shape)


def second_conv_kernel(
    index_hbm, hidden_hbm, before, after, stats, vectors, marked_hbm, weights_hbm,
    out, done, source, even, odd, weights, sem, index, index_sem, hidden_stage, hidden_sem, marked, marked_sem,
):
    capacity = marked.shape[0]
    indexing = Fetched(index_hbm, index, index_sem)
    hidden = Fetched(hidden_hbm, hidden_stage, hidden_sem)
    marking = Fetched(marked_hbm, marked, marked_sem)
    fetch = pltpu.make_async_copy(weights_hbm, weights, sem)
    fetch.start()
    done[...] = jnp.zeros(done.shape, f32)
    slope = stats[1:2, :] * vectors[2:3, :]
    shift = vectors[3:4, :] - stats[0:1, :] * slope

    def prepare(refs, k, slot):
        values = refs[0][k].astype(f32)
        pre = values * slope + shift
        put_slot(source, slot, jnp.where(values < MARK_LIMIT, pre * sigmoid(pre), 0.0))

    each_slot(capacity, (hidden,), (before,), (after,), prepare)
    put_slot(source, capacity + 2 * EDGE, jnp.zeros((128, 256), f32))
    marking.ready()
    indexing.ready()
    fetch.wait()

    def finish(b, total, carry):
        inputs = marked[b].astype(f32)
        out[b] = jnp.where(inputs < MARK_LIMIT, inputs + total, 0.0).astype(bf16)
        return carry

    conv(index, source, (even, odd), weights, False, capacity, finish, 0)


def back_conv_kernel(
    index_hbm, rows, hidden_hbm, hid_before, hid_after, grad, grad_before, grad_after,
    stats_second, marked_hbm, stats_first, vectors, cotangent, weights_hbm, after_conv,
    partial, normed_out, row, source, even, odd, weights, sem, index, index_sem, hidden_stage, hidden_sem, marked, marked_sem,
    stage, stage_sem,
):
    capacity = marked.shape[0]
    indexing = Fetched(index_hbm, index, index_sem)
    hidden = Fetched(hidden_hbm, hidden_stage, hidden_sem)
    marking = Fetched(marked_hbm, marked, marked_sem)
    fetch = pltpu.make_async_copy(weights_hbm, weights, sem)
    fetch.start()
    own = Fetched(cotangent, stage, stage_sem)
    mean, inv_scale, voxel_total = (stats_second[k : k + 1, :] for k in range(3))
    first, second = combine_pairs(rows[...], voxel_total)
    gains, biases = vectors[2:3, :], vectors[3:4, :]

    def prepare(refs, k, slot):
        values = refs[0][k].astype(f32)
        normed = (values - mean) * inv_scale
        scaled = refs[1][k].astype(f32) * slope_of(normed * gains + biases) * gains
        result = inv_scale * (scaled - first - normed * second)
        put_slot(source, slot, jnp.where(values < MARK_LIMIT, result, 0.0))

    each_slot(capacity, (hidden, grad), (hid_before, grad_before), (hid_after, grad_after), prepare)
    put_slot(source, capacity + 2 * EDGE, jnp.zeros((128, 256), f32))
    marking.ready()
    indexing.ready()
    fetch.wait()
    own.ready()
    mean_first, inv_first = stats_first[0:1, :], stats_first[1:2, :]
    gains_first, biases_first = vectors[0:1, :], vectors[1:2, :]

    def finish(b, total, carry):
        values = marked[b].astype(f32)
        normed = (values - mean_first) * inv_first
        on = values < MARK_LIMIT
        scaled = total * slope_of(normed * gains_first + biases_first) * gains_first
        scaled = jnp.where(on, scaled, 0.0)
        normed = jnp.where(on, normed, 0.0)
        whole = stage[b].astype(f32) + inv_first * scaled
        partial[b] = jnp.where(on, whole, MARK)
        normed_out[b] = normed
        return carry[0] + eight_rows(scaled), carry[1] + eight_rows(scaled * normed)

    zero = jnp.zeros((8, 256), f32)
    sums = conv(index, source, (even, odd), weights, True, capacity, finish, (zero, zero))
    row[...] = jnp.broadcast_to(pairs_row(column_sum(sums[0]), column_sum(sums[1])), row.shape)


def end_kernel(rows, partial, normed, stats, out_hbm, out, sem):
    capacity = partial.shape[0]
    inv_scale, voxel_total = stats[1:2, :], stats[2:3, :]
    first, second = combine_pairs(rows[...], voxel_total)
    first, second = inv_scale * first, inv_scale * second

    def done(b):
        return pltpu.make_async_copy(out.at[b], out_hbm.at[b], sem.at[b])

    def step(b, carry):
        whole = partial[b]
        out[b] = jnp.where(whole < MARK_LIMIT, whole - first - normed[b] * second, 0.0).astype(bf16)
        done(b).start()
        return carry

    lax.fori_loop(0, capacity, step, 0)
    for b in range(capacity):
        done(b).wait()


def on_device(
    features, voxel_mask, counts, neighbors, w_first, w_second,
    gain_first, bias_first, gain_second, bias_second, cotangent,
):
    capacity, voxels, channels = features.shape
    devices = counts.shape[0]
    vectors = [v.reshape(1, channels) for v in (gain_first, bias_first, gain_second, bias_second)]
    gain_first, bias_first, gain_second, bias_second = vectors
    w_first = w_first.reshape(27, channels, channels)
    w_second = w_second.reshape(27, channels, channels)

    def shift_up(x):
        return lax.ppermute(x, AXES, [(i, (i + 1) % devices) for i in range(devices)])

    def shift_down(x):
        return lax.ppermute(x, AXES, [((i + 1) % devices, i) for i in range(devices)])

    def exchange(row):
        return lax.all_to_all(row, AXES, 0, 0, tiled=True)

    whole = ((capacity, voxels, channels), bf16)
    whole_wide = ((capacity, voxels, channels), f32)
    table = (neighbors.shape, jnp.int32)
    edge = ((EDGE, voxels, channels), bf16)
    packed = ((devices, 128), f32)
    vector = ((8, channels), f32)
    slots = capacity + 2 * EDGE + 1

    dma = pltpu.SemaphoreType.DMA
    marked_near, feat_up, feat_down, cot_up, cot_down, vectors, index = call(
        mark_kernel, "mark", [hbm()] * 9,
        [whole, edge, edge, edge, edge, vector, (*table, "hbm")],
        [
            pltpu.VMEM(*table), dma, pltpu.VMEM(*table), dma,
            pltpu.VMEM(*whole), pltpu.VMEM((2 * EDGE, voxels, channels), bf16), dma((2 * EDGE,)),
            pltpu.VMEM((capacity, voxels), jnp.int32),
            pltpu.VMEM((4, 1, channels), f32),
            dma((capacity,)), dma((5,)), pltpu.SMEM(counts.shape, jnp.int32), dma,
        ],
    )(counts, neighbors, features, voxel_mask, cotangent, gain_first, bias_first, gain_second, bias_second)
    cot_before, cot_after = shift_up(cot_up), shift_down(cot_down)
    feat_before, feat_after = shift_up(feat_up), shift_down(feat_down)
    row, marked = call(
        first_sums_kernel, "first_sums", [vmem()], [packed, (*whole, "hbm")], [dma]
    )(marked_near)
    rows_first = exchange(row)

    (grad,) = call(
        grad_conv_kernel, "grad_conv", [hbm(), hbm(), hbm(), vmem(), vmem(), hbm()],
        [whole_wide], conv_scratch(slots, capacity) + [pltpu.VMEM(*whole), dma] * 2,
    )(index, cotangent, marked, cot_before, cot_after, w_second)

    hidden_near, row, hid_up, hid_down, stats_first = call(
        first_conv_kernel, "first_conv",
        [hbm(), hbm(), vmem(), hbm(), vmem(), vmem(), vmem(), hbm()],
        [whole, packed, edge, edge, vector],
        conv_scratch(slots, capacity)
        + [
            pltpu.VMEM(*whole), dma, pltpu.SMEM(counts.shape, jnp.int32), dma,
        ],
    )(index, counts, rows_first, marked, feat_before, feat_after, vectors, w_first)
    rows_second = exchange(row)
    hid_before, hid_after = shift_up(hid_up), shift_down(hid_down)

    row, stats_second, grad_up, grad_down, hidden = call(
        second_sums_kernel, "second_sums", [hbm()] + [vmem()] * 4, [packed, vector, edge, edge, (*whole, "hbm")],
        [pltpu.SMEM(counts.shape, jnp.int32), dma, dma],
    )(
        counts, rows_second, hidden_near, grad, vectors
    )
    grad_before, grad_after = shift_up(grad_up), shift_down(grad_down)
    rows_third = exchange(row)

    output, done = call(
        second_conv_kernel, "second_conv", [hbm(), hbm(), vmem(), vmem(), vmem(), vmem(), hbm(), hbm()],
        [whole, ((8, 128), f32)],
        conv_scratch(slots, capacity) + [pltpu.VMEM(*whole), dma, pltpu.VMEM(*whole), dma],
    )(index, hidden, hid_before, hid_after, stats_second, vectors, marked, w_second)

    partial, normed, row = call(
        back_conv_kernel, "back_conv", [hbm(), vmem(), hbm()] + [vmem()] * 6 + [hbm(), vmem(), vmem(), hbm(), hbm(), vmem()],
        [whole_wide, whole_wide, packed],
        conv_scratch(slots, capacity) + [pltpu.VMEM(*whole), dma] * 3,
    )(
        index, rows_third, hidden, hid_before, hid_after, grad, grad_before, grad_after,
        stats_second, marked, stats_first, vectors, cotangent, w_first, done,
    )
    rows_fourth = exchange(row)

    (grad_features,) = call(
        end_kernel, "end", [vmem()] * 4, [(*whole, "hbm")], [pltpu.VMEM(*whole), dma((capacity,))]
    )(rows_fourth, partial, normed, stats_first)
    return (output, grad_features)


def solution(mesh):
    split = P(AXES, None, None)
    placed = (split, P(AXES, None), P(), P(AXES, None), P(), P(), P(), P(), P(), P(), split)
    return jax.shard_map(
        on_device, mesh=mesh, in_specs=placed, out_specs=(split, split), check_vma=False
    )
```

```python
import functools

import jax
import jax.numpy as jnp
from jax import lax
from jax.experimental import pallas as pl
from jax.experimental.pallas import tpu as pltpu
from jax.sharding import PartitionSpec as P

GC = 8
EDGE = 3
AXES = ("region", "sub")
eps_norm = 1e-05
MARK = 2.0**100
MARK_LIMIT = 2.0**90
VMEM_LIMIT = 20 * 2**20
COSTS = {"second_sums": 50, "second_conv": 8, "first_conv": 8}
f32 = jnp.float32
bf16 = jnp.bfloat16


def vmem():
    return pl.BlockSpec(memory_space=pltpu.VMEM)


def hbm():
    return pl.BlockSpec(memory_space=pltpu.HBM)


def call(kernel, name, in_specs, outs, scratch=()):
    made = pl.pallas_call(
        kernel,
        name=name,
        in_specs=in_specs,
        out_specs=[hbm() if len(o) == 3 else vmem() for o in outs],
        out_shape=[pltpu.HBM(*o[:2]) if len(o) == 3 else jax.ShapeDtypeStruct(*o) for o in outs],
        scratch_shapes=list(scratch),
        cost_estimate=pl.CostEstimate(flops=int(COSTS[name] * 1.15e9), bytes_accessed=0, transcendentals=0)
        if name in COSTS
        else None,
        compiler_params=pltpu.CompilerParams(vmem_limit_bytes=VMEM_LIMIT),
    )

    def run(*operands):
        return made(
            *(
                pltpu.with_memory_space_constraint(x, pltpu.HBM)
                if spec.memory_space == pltpu.HBM
                else x
                for spec, x in zip(in_specs, operands)
            )
        )

    return run


class Fetched:
    def __init__(self, source, target, sem):
        self.copy = pltpu.make_async_copy(source, target, sem)
        self.copy.start()
        self.target = target

    def ready(self):
        self.copy.wait()
        return self.target


def lane_of(shape):
    return lax.broadcasted_iota(jnp.int32, shape, len(shape) - 1) % GC


def spread_first(x):
    x = jnp.where(lane_of(x.shape) == 0, x, 0.0)
    for s in (1, 2, 4):
        x = x + pltpu.roll(x, s, 1)
    return x


def group_total(x):
    for s in (1, 2, 4):
        x = x + pltpu.roll(x, 128 - s, 1)
    return spread_first(x)


def halves(x):
    return x[:, :128], x[:, 128:]


def pack_row(values):
    lane = lane_of((1, 128))
    row = jnp.zeros((1, 128), f32)
    for k, value in enumerate(values):
        row = jnp.where(lane == k, value, row)
    return row


def unpack_row(rows, k):
    return spread_first(pltpu.roll(rows, 128 - k, 1) if k else rows)


def join(pair):
    return jnp.concatenate(pair, axis=1)


def column_sum(x):
    return jnp.sum(x, axis=0, keepdims=True)


def no_moments():
    zero = jnp.zeros((8, 256), f32)
    return zero, zero, zero, zero[:, :128]


def add_moments(moments, values, on, first):
    base, sums, squares, count = moments
    here = eight_rows(jnp.where(on[:, :128], 1.0, 0.0))
    number = jnp.maximum(here, 1.0)
    base = jnp.where(first, eight_rows(jnp.where(on, values, 0.0)) / join([number, number]), base)
    apart = jnp.where(on.reshape(16, 8, 256), values.reshape(16, 8, 256) - base, 0.0)
    sums = sums + jnp.sum(apart, axis=0)
    squares = squares + jnp.sum(apart * apart, axis=0)
    return base, sums, squares, count + here


def moments_row(moments):
    base, total, square, count = moments
    safe = jnp.maximum(count, 1.0)
    number = column_sum(count)
    sums, squares = [], []
    for base, total, square in zip(halves(base), halves(total), halves(square)):
        apart = total / safe
        mean = base + apart
        group_sum = group_total(column_sum(count * mean))
        group_mean = group_sum / jnp.maximum(number * float(GC), 1.0)
        about = square - total * apart + count * ((mean - group_mean) * (mean - group_mean))
        sums.append(group_sum)
        squares.append(group_total(column_sum(about)))
    return pack_row([*sums, *squares, number * float(GC)])


def combine_moments(rows):
    count = unpack_row(rows, 4)
    total = column_sum(count)
    safe = jnp.maximum(count, 1.0)
    means, scales = [], []
    for k in (0, 1):
        sums = unpack_row(rows, k)
        mean = column_sum(sums) / total
        apart = sums / safe - mean
        spread = column_sum(unpack_row(rows, 2 + k) + count * (apart * apart)) / total
        means.append(mean)
        scales.append(lax.rsqrt(spread + eps_norm))
    return join(means), join(scales), join([total, total])


def combine_pairs(rows, total):
    summed = column_sum(rows)
    first = join([unpack_row(summed, 0), unpack_row(summed, 1)]) / total
    second = join([unpack_row(summed, 2), unpack_row(summed, 3)]) / total
    return first, second


def pairs_row(first, second):
    return pack_row([group_total(h) for h in (*halves(first), *halves(second))])


def eight_rows(x):
    return jnp.sum(x.reshape(16, 8, x.shape[-1]), axis=0)


def put_slot(source, slot, values):
    tile = values.reshape(16, 8, 256)
    source[1, slot] = tile
    source[0, slot] = pltpu.roll(tile, 1, 1)
    source[2, slot] = pltpu.roll(tile, 7, 1)


def build(index, brick, source, windows):
    z = lax.broadcasted_iota(jnp.int32, (1, 8, 256), 1)
    for slab in range(6):
        dx, x = (0, 3) if slab == 0 else (2, 0) if slab == 5 else (1, slab - 1)
        for l in range(3):
            parts = []
            for dy, y, n in ((0, 3, 1), (1, 0, 4), (2, 0, 1)):
                at = pl.ds(x * 4 + y, n)
                part = source[l, index[brick, dx * 9 + dy * 3 + 1], at]
                if l != 1:
                    edge = source[l, index[brick, dx * 9 + dy * 3 + l], at]
                    part = jnp.where(z == (0 if l == 0 else 7), edge, part)
                parts.append(part)
            columns = jnp.concatenate(parts, axis=0)
            for j in range(3):
                windows[j * 3 + l, slab * 32 : slab * 32 + 32, :] = (
                    columns[j : j + 4].reshape(32, 256).astype(bf16)
                )


def product(pair, weights, backward):
    total = None
    for i in range(3):
        for j in range(3):
            for l in range(3):
                o = i * 9 + j * 3 + l
                taken = jnp.concatenate(
                    [pair[k, j * 3 + l, i * 32 : i * 32 + 128, :] for k in range(2)], axis=0
                )
                if backward:
                    part = lax.dot_general(
                        taken, weights[26 - o], (((1,), (1,)), ((), ())), preferred_element_type=f32
                    )
                else:
                    part = jnp.dot(taken, weights[o], preferred_element_type=f32)
                total = part if total is None else total + part
    return total


def conv(index, source, pairs, weights, backward, capacity, finish, carry):
    even, odd = pairs

    def build_pair(first, pair):
        first = jnp.minimum(first, capacity - 2)
        for k in range(2):
            build(index, first + k, source, pair.at[k])

    def finish_pair(first, pair, carry):
        both = product(pair, weights, backward)
        carry = finish(first, both[:128], carry)
        return finish(first + 1, both[128:], carry)

    build_pair(0, even)

    def four(step, carry):
        first = 4 * step
        build_pair(first + 2, odd)
        carry = finish_pair(first, even, carry)
        build_pair(first + 4, even)
        return finish_pair(first + 2, odd, carry)

    return lax.fori_loop(0, capacity // 4, four, carry)


def conv_scratch(slots, capacity):
    return [
        pltpu.VMEM((3, slots, 16, 8, 256), f32),
        pltpu.VMEM((2, 9, 192, 256), bf16),
        pltpu.VMEM((2, 9, 192, 256), bf16),
        pltpu.VMEM((27, 256, 256), bf16),
        pltpu.SemaphoreType.DMA,
        pltpu.SMEM((capacity, 27), jnp.int32),
        pltpu.SemaphoreType.DMA,
    ]


def each_slot(capacity, own, before, after, body):
    def run(refs, start, count):
        def step(k, _):
            body(refs, k, start + k)
            return 0

        lax.fori_loop(0, count, step, 0)

    run(before, capacity, EDGE)
    run(after, capacity + EDGE, EDGE)
    run([x.ready() if isinstance(x, Fetched) else x for x in own], 0, capacity)


def sigmoid(x):
    return 1.0 / (1.0 + jnp.exp(-x))


def mark_kernel(
    counts_hbm, neighbors_hbm, features, mask, cotangent, gain_first, bias_first, gain_second, bias_second,
    marked, feat_up, feat_down, cot_up, cot_down, vectors, index_hbm,
    neighbors, neighbors_sem, index, index_sem,
    stage, cot_stage, cot_sem, mask_stage, vector_stage, feature_sem, small_sem, counts, counts_sem,
):
    capacity = marked.shape[0]
    counting = Fetched(counts_hbm, counts, counts_sem)
    naming = Fetched(neighbors_hbm, neighbors, neighbors_sem)
    small = [pltpu.make_async_copy(mask, mask_stage, small_sem.at[0])]
    for k, vector in enumerate((gain_first, bias_first, gain_second, bias_second)):
        small.append(pltpu.make_async_copy(vector, vector_stage.at[k], small_sem.at[k + 1]))

    def arriving(b):
        return pltpu.make_async_copy(features.at[b], stage.at[b], feature_sem.at[b])

    for copy in small + [arriving(b) for b in range(capacity)]:
        copy.start()
    device = lax.axis_index(AXES)
    live = counting.ready()[device]
    edges = []
    for k in range(EDGE):
        for at, brick in ((k, live - EDGE + k), (EDGE + k, k)):
            edges.append(pltpu.make_async_copy(cotangent.at[brick], cot_stage.at[at], cot_sem.at[at]))
    for copy in edges:
        copy.start()

    live_before = counts[jnp.maximum(device - 1, 0)]
    named = naming.ready()[...]
    owner = lax.div(named, capacity)
    within = named - owner * capacity
    slot = jnp.where(
        owner == device,
        within,
        jnp.where(
            owner == device - 1, within + (capacity + EDGE - live_before), within + (capacity + EDGE)
        ),
    )
    index[...] = jnp.where(named < 0, capacity + 2 * EDGE, slot)
    indexed = pltpu.make_async_copy(index, index_hbm, index_sem)
    indexed.start()

    small[0].wait()
    def step(b, _):
        wide = jnp.broadcast_to(mask_stage[pl.ds(b, 1), :].astype(f32), (128, 128)).T
        wide = wide * jnp.where(b < live, 1.0, 0.0)
        arriving(b).wait()
        marked[b] = jnp.where(join([wide, wide]) > 0.5, stage[b].astype(f32), MARK).astype(bf16)
        return 0

    lax.fori_loop(0, capacity, step, 0, unroll=4)
    for copy in edges:
        copy.wait()
    for k in range(EDGE):
        for feat, cot, at, brick in (
            (feat_up, cot_up, k, live - EDGE + k), (feat_down, cot_down, EDGE + k, k)
        ):
            values = marked[brick]
            feat[k] = values
            on = values.astype(f32) < MARK_LIMIT
            cot[k] = jnp.where(on, cot_stage[at].astype(f32), 0.0).astype(bf16)
    indexed.wait()
    for copy in small[1:]:
        copy.wait()
    for k in range(4):
        vectors[k : k + 1, :] = vector_stage[k]
    vectors[4:8, :] = jnp.zeros((4, 256), f32)


def first_sums_kernel(marked, row, marked_hbm, out_sem):
    kept = pltpu.make_async_copy(marked, marked_hbm, out_sem)
    kept.start()
    capacity = marked.shape[0]


    def step(b, moments):
        values = marked[b].astype(f32)
        return add_moments(moments, values, values < MARK_LIMIT, b == 0)

    moments = lax.fori_loop(0, capacity, step, no_moments(), unroll=4)
    row[...] = jnp.broadcast_to(moments_row(moments), row.shape)
    kept.wait()


def grad_conv_kernel(
    index_hbm, cotangent, marked, before, after, weights_hbm,
    grad, source, even, odd, weights, sem, index, index_sem, stage, stage_sem,
):
    capacity = marked.shape[0]
    indexing = Fetched(index_hbm, index, index_sem)
    own = Fetched(cotangent, stage, stage_sem)
    fetch = pltpu.make_async_copy(weights_hbm, weights, sem)
    fetch.start()
    for k in range(EDGE):
        put_slot(source, capacity + k, before[k].astype(f32))
        put_slot(source, capacity + EDGE + k, after[k].astype(f32))
    put_slot(source, capacity + 2 * EDGE, jnp.zeros((128, 256), f32))
    own.ready()

    def own_slot(b, _):
        values = stage[b].astype(f32)
        put_slot(source, b, jnp.where(marked[b].astype(f32) < MARK_LIMIT, values, 0.0))
        return 0

    lax.fori_loop(0, capacity, own_slot, 0)
    indexing.ready()
    fetch.wait()

    def finish(b, total, carry):
        grad[b] = total
        return carry

    conv(index, source, (even, odd), weights, True, capacity, finish, 0)


def first_conv_kernel(
    index_hbm, counts_hbm, rows, marked, before, after, vectors, weights_hbm,
    hidden, row, up, down, stats, source, even, odd, weights, sem, index, index_sem,
    counts, counts_sem,
):
    capacity = hidden.shape[0]
    indexing = Fetched(index_hbm, index, index_sem)
    counting = Fetched(counts_hbm, counts, counts_sem)
    fetch = pltpu.make_async_copy(weights_hbm, weights, sem)
    fetch.start()
    mean, inv_scale, voxel_total = combine_moments(rows[...])
    stats[...] = jnp.concatenate(
        [mean, inv_scale, voxel_total, jnp.zeros((5, 256), f32)], axis=0
    )
    slope = inv_scale * vectors[0:1, :]
    shift = vectors[1:2, :] - mean * slope

    def prepare(refs, k, slot):
        values = refs[0][k].astype(f32)
        pre = values * slope + shift
        put_slot(source, slot, jnp.where(values < MARK_LIMIT, pre * sigmoid(pre), 0.0))

    each_slot(capacity, (marked,), (before,), (after,), prepare)
    put_slot(source, capacity + 2 * EDGE, jnp.zeros((128, 256), f32))
    indexing.ready()
    fetch.wait()

    def finish(b, total, carry):
        on = marked[b].astype(f32) < MARK_LIMIT
        rounded = total.astype(bf16).astype(f32)
        hidden[b] = jnp.where(on, rounded, MARK).astype(bf16)
        return add_moments(carry, rounded, on, b == 0)

    moments = conv(index, source, (even, odd), weights, False, capacity, finish, no_moments())
    live = counting.ready()[lax.axis_index(AXES)]
    for k in range(EDGE):
        up[k] = hidden[live - EDGE + k]
        down[k] = hidden[k]
    row[...] = jnp.broadcast_to(moments_row(moments), row.shape)


def slope_of(pre):
    part = sigmoid(pre)
    return part * (1.0 + pre * (1.0 - part))


def second_sums_kernel(counts_hbm, rows, hidden, grad, vectors, row, stats, up, down, hidden_hbm, counts, counts_sem, out_sem):
    counting = Fetched(counts_hbm, counts, counts_sem)
    kept = pltpu.make_async_copy(hidden, hidden_hbm, out_sem)
    kept.start()
    capacity = hidden.shape[0]
    mean, inv_scale, voxel_total = combine_moments(rows[...])
    stats[...] = jnp.concatenate(
        [mean, inv_scale, voxel_total, jnp.zeros((5, 256), f32)], axis=0
    )
    gains, biases = vectors[2:3, :], vectors[3:4, :]

    def step(b, carry):
        values = hidden[b].astype(f32)
        normed = (values - mean) * inv_scale
        scaled = grad[b] * slope_of(normed * gains + biases) * gains
        on = values < MARK_LIMIT
        scaled = jnp.where(on, scaled, 0.0)
        normed = jnp.where(on, normed, 0.0)
        return carry[0] + eight_rows(scaled), carry[1] + eight_rows(scaled * normed)

    zero = jnp.zeros((8, 256), f32)
    first, second = lax.fori_loop(0, capacity, step, (zero, zero), unroll=2)
    live = counting.ready()[lax.axis_index(AXES)]
    for k in range(EDGE):
        up[k] = grad[live - EDGE + k].astype(bf16)
        down[k] = grad[k].astype(bf16)
    kept.wait()
    row[...] = jnp.broadcast_to(pairs_row(column_sum(first), column_sum(second)), row.shape)


def second_conv_kernel(
    index_hbm, hidden_hbm, before, after, stats, vectors, marked_hbm, weights_hbm,
    out, done, source, even, odd, weights, sem, index, index_sem, hidden_stage, hidden_sem, marked, marked_sem,
):
    capacity = marked.shape[0]
    indexing = Fetched(index_hbm, index, index_sem)
    hidden = Fetched(hidden_hbm, hidden_stage, hidden_sem)
    marking = Fetched(marked_hbm, marked, marked_sem)
    fetch = pltpu.make_async_copy(weights_hbm, weights, sem)
    fetch.start()
    done[...] = jnp.zeros(done.shape, f32)
    slope = stats[1:2, :] * vectors[2:3, :]
    shift = vectors[3:4, :] - stats[0:1, :] * slope

    def prepare(refs, k, slot):
        values = refs[0][k].astype(f32)
        pre = values * slope + shift
        put_slot(source, slot, jnp.where(values < MARK_LIMIT, pre * sigmoid(pre), 0.0))

    each_slot(capacity, (hidden,), (before,), (after,), prepare)
    put_slot(source, capacity + 2 * EDGE, jnp.zeros((128, 256), f32))
    marking.ready()
    indexing.ready()
    fetch.wait()

    def finish(b, total, carry):
        inputs = marked[b].astype(f32)
        out[b] = jnp.where(inputs < MARK_LIMIT, inputs + total, 0.0).astype(bf16)
        return carry

    conv(index, source, (even, odd), weights, False, capacity, finish, 0)


def back_conv_kernel(
    index_hbm, rows, hidden_hbm, hid_before, hid_after, grad, grad_before, grad_after,
    stats_second, marked_hbm, stats_first, vectors, cotangent, weights_hbm, after_conv,
    partial, normed_out, row, source, even, odd, weights, sem, index, index_sem, hidden_stage, hidden_sem, marked, marked_sem,
    stage, stage_sem,
):
    capacity = marked.shape[0]
    indexing = Fetched(index_hbm, index, index_sem)
    hidden = Fetched(hidden_hbm, hidden_stage, hidden_sem)
    marking = Fetched(marked_hbm, marked, marked_sem)
    fetch = pltpu.make_async_copy(weights_hbm, weights, sem)
    fetch.start()
    own = Fetched(cotangent, stage, stage_sem)
    mean, inv_scale, voxel_total = (stats_second[k : k + 1, :] for k in range(3))
    first, second = combine_pairs(rows[...], voxel_total)
    gains, biases = vectors[2:3, :], vectors[3:4, :]

    def prepare(refs, k, slot):
        values = refs[0][k].astype(f32)
        normed = (values - mean) * inv_scale
        scaled = refs[1][k].astype(f32) * slope_of(normed * gains + biases) * gains
        result = inv_scale * (scaled - first - normed * second)
        put_slot(source, slot, jnp.where(values < MARK_LIMIT, result, 0.0))

    each_slot(capacity, (hidden, grad), (hid_before, grad_before), (hid_after, grad_after), prepare)
    put_slot(source, capacity + 2 * EDGE, jnp.zeros((128, 256), f32))
    marking.ready()
    indexing.ready()
    fetch.wait()
    own.ready()
    mean_first, inv_first = stats_first[0:1, :], stats_first[1:2, :]
    gains_first, biases_first = vectors[0:1, :], vectors[1:2, :]

    def finish(b, total, carry):
        values = marked[b].astype(f32)
        normed = (values - mean_first) * inv_first
        on = values < MARK_LIMIT
        scaled = total * slope_of(normed * gains_first + biases_first) * gains_first
        scaled = jnp.where(on, scaled, 0.0)
        normed = jnp.where(on, normed, 0.0)
        whole = stage[b].astype(f32) + inv_first * scaled
        partial[b] = jnp.where(on, whole, MARK)
        normed_out[b] = normed
        return carry[0] + eight_rows(scaled), carry[1] + eight_rows(scaled * normed)

    zero = jnp.zeros((8, 256), f32)
    sums = conv(index, source, (even, odd), weights, True, capacity, finish, (zero, zero))
    row[...] = jnp.broadcast_to(pairs_row(column_sum(sums[0]), column_sum(sums[1])), row.shape)


def end_kernel(rows, partial, normed, stats, out_hbm, out, sem):
    capacity = partial.shape[0]
    inv_scale, voxel_total = stats[1:2, :], stats[2:3, :]
    first, second = combine_pairs(rows[...], voxel_total)
    first, second = inv_scale * first, inv_scale * second

    def done(b):
        return pltpu.make_async_copy(out.at[b], out_hbm.at[b], sem.at[b])

    def step(b, carry):
        whole = partial[b]
        out[b] = jnp.where(whole < MARK_LIMIT, whole - first - normed[b] * second, 0.0).astype(bf16)
        done(b).start()
        return carry

    lax.fori_loop(0, capacity, step, 0)
    for b in range(capacity):
        done(b).wait()


def on_device(
    features, voxel_mask, counts, neighbors, w_first, w_second,
    gain_first, bias_first, gain_second, bias_second, cotangent,
):
    capacity, voxels, channels = features.shape
    devices = counts.shape[0]
    vectors = [v.reshape(1, channels) for v in (gain_first, bias_first, gain_second, bias_second)]
    gain_first, bias_first, gain_second, bias_second = vectors
    w_first = w_first.reshape(27, channels, channels)
    w_second = w_second.reshape(27, channels, channels)

    def shift_up(x):
        return lax.ppermute(x, AXES, [(i, (i + 1) % devices) for i in range(devices)])

    def shift_down(x):
        return lax.ppermute(x, AXES, [((i + 1) % devices, i) for i in range(devices)])

    def exchange(row):
        return lax.all_to_all(row, AXES, 0, 0, tiled=True)

    whole = ((capacity, voxels, channels), bf16)
    whole_wide = ((capacity, voxels, channels), f32)
    table = (neighbors.shape, jnp.int32)
    edge = ((EDGE, voxels, channels), bf16)
    packed = ((devices, 128), f32)
    vector = ((8, channels), f32)
    slots = capacity + 2 * EDGE + 1

    dma = pltpu.SemaphoreType.DMA
    marked_near, feat_up, feat_down, cot_up, cot_down, vectors, index = call(
        mark_kernel, "mark", [hbm()] * 9,
        [whole, edge, edge, edge, edge, vector, (*table, "hbm")],
        [
            pltpu.VMEM(*table), dma, pltpu.VMEM(*table), dma,
            pltpu.VMEM(*whole), pltpu.VMEM((2 * EDGE, voxels, channels), bf16), dma((2 * EDGE,)),
            pltpu.VMEM((capacity, voxels), jnp.int32),
            pltpu.VMEM((4, 1, channels), f32),
            dma((capacity,)), dma((5,)), pltpu.SMEM(counts.shape, jnp.int32), dma,
        ],
    )(counts, neighbors, features, voxel_mask, cotangent, gain_first, bias_first, gain_second, bias_second)
    cot_before, cot_after = shift_up(cot_up), shift_down(cot_down)
    feat_before, feat_after = shift_up(feat_up), shift_down(feat_down)
    row, marked = call(
        first_sums_kernel, "first_sums", [vmem()], [packed, (*whole, "hbm")], [dma]
    )(marked_near)
    rows_first = exchange(row)

    (grad,) = call(
        grad_conv_kernel, "grad_conv", [hbm(), hbm(), vmem(), vmem(), vmem(), hbm()],
        [whole_wide], conv_scratch(slots, capacity) + [pltpu.VMEM(*whole), dma],
    )(index, cotangent, marked_near, cot_before, cot_after, w_second)

    hidden_near, row, hid_up, hid_down, stats_first = call(
        first_conv_kernel, "first_conv",
        [hbm(), hbm(), vmem(), vmem(), vmem(), vmem(), vmem(), hbm()],
        [whole, packed, edge, edge, vector],
        conv_scratch(slots, capacity)
        + [
            pltpu.SMEM(counts.shape, jnp.int32), dma,
        ],
    )(index, counts, rows_first, marked_near, feat_before, feat_after, vectors, w_first)
    rows_second = exchange(row)
    hid_before, hid_after = shift_up(hid_up), shift_down(hid_down)

    row, stats_second, grad_up, grad_down, hidden = call(
        second_sums_kernel, "second_sums", [hbm()] + [vmem()] * 4, [packed, vector, edge, edge, (*whole, "hbm")],
        [pltpu.SMEM(counts.shape, jnp.int32), dma, dma],
    )(
        counts, rows_second, hidden_near, grad, vectors
    )
    grad_before, grad_after = shift_up(grad_up), shift_down(grad_down)
    rows_third = exchange(row)

    output, done = call(
        second_conv_kernel, "second_conv", [hbm(), hbm(), vmem(), vmem(), vmem(), vmem(), hbm(), hbm()],
        [whole, ((8, 128), f32)],
        conv_scratch(slots, capacity) + [pltpu.VMEM(*whole), dma, pltpu.VMEM(*whole), dma],
    )(index, hidden, hid_before, hid_after, stats_second, vectors, marked, w_second)

    partial, normed, row = call(
        back_conv_kernel, "back_conv", [hbm(), vmem(), hbm()] + [vmem()] * 6 + [hbm(), vmem(), vmem(), hbm(), hbm(), vmem()],
        [whole_wide, whole_wide, packed],
        conv_scratch(slots, capacity) + [pltpu.VMEM(*whole), dma] * 3,
    )(
        index, rows_third, hidden, hid_before, hid_after, grad, grad_before, grad_after,
        stats_second, marked, stats_first, vectors, cotangent, w_first, done,
    )
    rows_fourth = exchange(row)

    (grad_features,) = call(
        end_kernel, "end", [vmem()] * 4, [(*whole, "hbm")], [pltpu.VMEM(*whole), dma((capacity,))]
    )(rows_fourth, partial, normed, stats_first)
    return (output, grad_features)


def solution(mesh):
    split = P(AXES, None, None)
    placed = (split, P(AXES, None), P(), P(AXES, None), P(), P(), P(), P(), P(), P(), split)
    return jax.shard_map(
        on_device, mesh=mesh, in_specs=placed, out_specs=(split, split), check_vma=False
    )
```
